128 devices in a mesh: lib: 16 (over z, y), lmk: 8 (over x, core).
Axes of the slice: x: 4, y: 4, z: 4, core: 2. Of those that a mesh axis runs over, the one named last changes fastest.
Arguments:
- library_bits: bfloat16 [12288, 2048], P('lib'), may hold values from 0 to 1, as said below
- library_count: int32 [12288], P('lib'), may hold values from 1 to 2048, as said below
- landmark_bits: bfloat16 [8192, 2048], P('lmk'), may hold values from 0 to 1, as said below
- landmark_count: int32 [8192], P('lmk'), may hold values from 1 to 2048, as said below
- inverse_root: bfloat16 [8192, 8192], P('lib', 'lmk'), may hold values from -0.09375 to 0.09375
Outputs:
- features: float32 [12288, 8192], P('lib', 'lmk')
The draws below stay inside these ranges and needn't reach their ends.
Inputs may be any that keep to these rules, and one draw needn't show every extreme that they name: `library_bits`: every entry is 0 or 1; every fingerprint has at least one set bit, one has all 2048 set and one has exactly one. `library_count`: the number of ones in the same row of library_bits. `landmark_bits`: every entry is 0 or 1; every fingerprint has at least one set bit, one has all 2048 set and one has exactly one. `landmark_count`: the number of ones in the same row of landmark_bits.
All inputs are finite; a program needn't handle non-finite values.
Results may differ from the reference program's by a relative error of at most 0.0027.
Values may be sent and summed in bfloat16 or wider, within the bound.
No kernel may reach another device: no remote copies, remote signals or barrier semaphores. Data moves between devices by JAX's collectives and lax.ppermute only.
A program may use at most 128 MiB of HBM per device.

```python
import jax
import jax.numpy as jnp
from jax import lax

BITS = 2048
NLM = 8192
NLIB = 12288


def fingerprint(key, rows):
    levels = jax.random.randint(jax.random.fold_in(key, 11), (rows, 1), 5, 996)
    raw = jax.random.randint(jax.random.fold_in(key, 12), (rows, BITS), 0, 1000)
    bits = (raw < levels).astype(jnp.int32)
    place = jax.random.randint(jax.random.fold_in(key, 13), (rows, 1), 0, BITS)
    forced = (jnp.arange(BITS, dtype=jnp.int32)[None, :] == place).astype(jnp.int32)
    row_index = jnp.arange(rows, dtype=jnp.int32)[:, None]
    merged = jnp.maximum(bits, forced)
    merged = jnp.where(row_index == 1, forced, merged)
    merged = jnp.where(row_index == 0, jnp.ones_like(merged), merged)
    return merged


def draw_library_bits(key, part):
    bits = fingerprint(jax.random.fold_in(key, 101), NLIB)
    return bits.astype(jnp.float32).astype(jnp.bfloat16)


def draw_library_count(key, part):
    bits = fingerprint(jax.random.fold_in(key, 101), NLIB)
    return jnp.sum(bits, axis=1).astype(jnp.int32)


def draw_landmark_bits(key, part):
    bits = fingerprint(jax.random.fold_in(key, 202), NLM)
    return bits.astype(jnp.float32).astype(jnp.bfloat16)


def draw_landmark_count(key, part):
    bits = fingerprint(jax.random.fold_in(key, 202), NLM)
    return jnp.sum(bits, axis=1).astype(jnp.int32)


def raised(drawn, own_key, source, target, shards_of, factor):
    def block_of(position):
        return (jnp.arange(drawn.shape[position]) // (drawn.shape[position] // shards_of)).reshape((-1,) + (1,) * (drawn.ndim - 1 - position))

    first = jax.random.permutation(own_key, shards_of)[block_of(target)]
    far = (block_of(target) + shards_of // 2) % shards_of
    return jnp.where((block_of(source) == first) | (block_of(source) == far), factor * drawn, drawn)


def block_levels(rng, extent, cuts, low, largest):
    def one(dim, blocks):
        draws = jax.random.uniform(jax.random.fold_in(jax.random.fold_in(rng, 6), dim), (blocks,), jnp.float32, low / len(cuts), largest / len(cuts))
        return jnp.repeat(jnp.exp(draws), extent[dim] // blocks).reshape((-1,) + (1,) * (len(extent) - dim - 1))

    factor_of = one(*cuts[0])
    for cut in cuts[1:]:
        factor_of = factor_of * one(*cut)
    return factor_of


def bell_draw_with(rng, extent, width, limit, cuts, heavy, kind=jnp.bfloat16):
    values = width * jax.random.normal(rng, extent, jnp.float32)
    if cuts:
        values = values * block_levels(rng, extent, cuts, -0.22, 0.18)
    return jnp.clip(raised(values, jax.random.fold_in(rng, 3), *heavy), -limit, limit).astype(kind)


def setup_inputs(seed: int = 0) -> dict:
    splits = jax.random.split(jax.random.key(seed), 6)
    return {
        "library_bits": draw_library_bits(jax.random.fold_in(splits[5], 71), 0),
        "library_count": draw_library_count(jax.random.fold_in(splits[5], 71), 0),
        "landmark_bits": draw_landmark_bits(jax.random.fold_in(splits[5], 71), 0),
        "landmark_count": draw_landmark_count(jax.random.fold_in(splits[5], 71), 0),
        "inverse_root": bell_draw_with(splits[4], (NLM, NLM), NLM ** -0.5, 0.09375, ((0, 16), (1, 8)), (0, 1, 16, 2.0)),
    }


def tversky(row_bits, row_count, col_bits, col_count):
    common = lax.dot_general(row_bits, col_bits, (((1,), (1,)), ((), ())), preferred_element_type=jnp.float32)
    scale_sum = 0.9 * row_count.astype(jnp.float32)[:, None] + 0.1 * col_count.astype(jnp.float32)[None, :]
    return (common / scale_sum).astype(jnp.bfloat16)


def reference(library_bits, library_count, landmark_bits, landmark_count, inverse_root):
    kernel = tversky(library_bits, library_count, landmark_bits, landmark_count)
    return jnp.dot(kernel, inverse_root, preferred_element_type=jnp.float32)
```

```python
import functools

import jax
import jax.numpy as jnp
from jax import lax
from jax.experimental import pallas as pl
from jax.experimental.pallas import tpu as pltpu
from jax.sharding import PartitionSpec as P

AXES = ("lib", "lmk")
NZ, NY, NX, NC = 4, 4, 4, 2


def ring_pairs(axis):
    pairs = []
    for z in range(NZ):
        for y in range(NY):
            for x in range(NX):
                for c in range(NC):
                    step = 1 if c == 0 else -1
                    tz = (z + step) % NZ if axis == "z" else z
                    ty = (y + step) % NY if axis == "y" else y
                    pairs.append((((z * NY + y) * NX + x) * NC + c, ((tz * NY + ty) * NX + x) * NC + c))
    return pairs


def ring(block, axis):
    got = []
    for _ in range(3):
        block = lax.ppermute(block, AXES, ring_pairs(axis))
        got.append(block)
    return got


def tversky(row_bits, row_count, col_bits, col_count):
    common = lax.dot_general(
        row_bits, col_bits, (((1,), (1,)), ((), ())), preferred_element_type=jnp.float32
    )
    scale_sum = (
        0.9 * row_count.astype(jnp.float32)[:, None] + 0.1 * col_count.astype(jnp.float32)[None, :]
    )
    return (common / scale_sum).astype(jnp.bfloat16)


def group_kernel(stages, n_r, has_acc, col0, width, offs, k_ref, *refs):
    r_refs = refs[:n_r]
    refs = refs[n_r:]
    if has_acc:
        acc_ref, refs = refs[0], refs[1:]
    out_ref, kbuf, rbuf, acc, k_sems, r_sems, o_sems = refs
    rows = acc.shape[0]
    tile = 256
    if has_acc:
        acc_in = pltpu.make_async_copy(acc_ref.at[:, pl.ds(col0, width)], acc, o_sems.at[0])
        acc_in.start()
    pos, nk, nr, plan = 0, 0, 0, []
    for stage in stages:
        copies, start = [], pos
        for ki, n, parts in stage:
            off = pl.multiple_of(offs[ki], 256)
            copies.append(pltpu.make_async_copy(k_ref.at[:, pl.ds(off, n)], kbuf.at[:, pl.ds(pos, n)], k_sems.at[nk]))
            nk += 1
            for ri, row0, column, columns in parts:
                copies.append(
                    pltpu.make_async_copy(
                        r_refs[ri].at[pl.ds(row0, n), :],
                        rbuf.at[pl.ds(pos, n), pl.ds(column, columns)],
                        r_sems.at[nr],
                    )
                )
                nr += 1
            pos += n
        for cp in copies:
            cp.start()
        plan.append((start, pos, copies))
    if has_acc:
        acc_in.wait()
    outs = []
    for s, (lo, hi, copies) in enumerate(plan):
        for cp in copies:
            cp.wait()
        for t in range(0, rows, tile):
            part = jnp.dot(kbuf[t : t + tile, lo:hi], rbuf[lo:hi, :], preferred_element_type=jnp.float32)
            if s == 0 and not has_acc:
                acc[t : t + tile, :] = part
            else:
                acc[t : t + tile, :] += part
            if s == len(plan) - 1:
                cp = pltpu.make_async_copy(
                    acc.at[pl.ds(t, tile), :], out_ref.at[pl.ds(t, tile), pl.ds(col0, width)], o_sems.at[1 + t // tile]
                )
                cp.start()
                outs.append(cp)
    for cp in outs:
        cp.wait()


def group(stages, rs, offs, k, acc, col0, width, out_cols=1024):
    rows = k.shape[0]
    depth = sum(n for st in stages for _, n, _ in st)
    n_k = sum(len(st) for st in stages)
    n_r = sum(len(p) for st in stages for _, _, p in st)
    has_acc = acc is not None
    args = [offs, k, *rs] + ([acc] if has_acc else [])
    any_spec = pl.BlockSpec(memory_space=pl.ANY)
    return pl.pallas_call(
        functools.partial(group_kernel, stages, len(rs), has_acc, col0, width),
        out_shape=jax.ShapeDtypeStruct((rows, out_cols), jnp.float32),
        in_specs=[pl.BlockSpec(memory_space=pltpu.SMEM)] + [any_spec] * (len(args) - 1),
        out_specs=any_spec,
        scratch_shapes=[
            pltpu.VMEM((rows, depth), jnp.bfloat16),
            pltpu.VMEM((depth, width), jnp.bfloat16),
            pltpu.VMEM((rows, width), jnp.float32),
            pltpu.SemaphoreType.DMA((n_k,)),
            pltpu.SemaphoreType.DMA((n_r,)),
            pltpu.SemaphoreType.DMA((1 + -(-rows // 256),)),
        ],
        input_output_aliases={len(args) - 1: 0} if has_acc else {},
        compiler_params=pltpu.CompilerParams(vmem_limit_bytes=40 * 2**20),
        cost_estimate=pl.CostEstimate(
            flops=2 * rows * depth * width,
            bytes_accessed=2 * depth * (rows + width) + 4 * rows * width,
            transcendentals=0,
        ),
    )(*args)


def shards(library_bits, library_count, landmark_bits, landmark_count, inverse_root):
    block = tversky(library_bits, library_count, landmark_bits, landmark_count)
    k = lax.all_gather(block, "lmk", axis=1, tiled=True)

    lib = lax.axis_index("lib")
    z, y = lib // NY, lib % NY
    step = 1 - 2 * (lax.axis_index("lmk") % NC)
    offs = jnp.stack(
        [(((z - i * step) % NZ) * NY + (y - j * step) % NY) * 512 for i in range(4) for j in range(4)]
    ).astype(jnp.int32)
    offs = jnp.concatenate([offs, offs + 256])

    half = inverse_root.shape[1] // 2
    top = inverse_root.shape[0] // 2
    sides = []
    for s in range(2):
        own = inverse_root[:, s * half : (s + 1) * half]
        ys, zs = ring(own, "y"), ring(own, "z")
        a = ring(jnp.concatenate([b[:top] for b in ys]), "z")
        b = ring(jnp.concatenate([b[top:] for b in zs]), "y")
        sides.append((own, ys, zs, a, b))

    def a_stage(i, pick):
        return [(4 * i + j, top, [(p, (j - 1) * top, col, half) for p, col in pick]) for j in (1, 2, 3)]

    def b_stage(j, pick):
        return [(16 + 4 * i + j, top, [(p, (i - 1) * top, col, half) for p, col in pick]) for i in (1, 2, 3)]

    both = lambda i: [(i, 0), (i + 1, half)]
    rs, units = [inverse_root], [(0, 512, [(0, 0, 0, 2 * half)])]
    for d in range(3):
        for which, index in ((1, d + 1), (2, 4 * (d + 1))):
            units.append((index, 512, [(len(rs), 0, 0, half), (len(rs) + 1, 0, half, half)]))
            rs += [sides[0][which][d], sides[1][which][d]]
    stages = [units[:1], units[1:3], units[3:5], units[5:7]]
    p = len(rs)
    rs += [sides[0][3][0], sides[1][3][0], sides[0][4][0], sides[1][4][0]]
    stages += [a_stage(1, both(p)), b_stage(1, both(p + 2))]
    out = group(stages, rs, offs, k, None, 0, 2 * half)
    rs = [sides[0][3][1], sides[1][3][1], sides[0][4][1], sides[1][4][1]]
    out = group([a_stage(2, both(0)), b_stage(2, both(2))], rs, offs, k, out, 0, 2 * half)
    for s in range(2):
        rs = [sides[s][3][2], sides[s][4][2]]
        out = group([a_stage(3, [(0, 0)]), b_stage(3, [(1, 0)])], rs, offs, k, out, s * half, half)
    return out


def solution(mesh):
    placed = (P("lib", None), P("lib"), P("lmk", None), P("lmk"), P("lib", "lmk"))
    return jax.shard_map(
        shards, mesh=mesh, in_specs=placed, out_specs=P("lib", "lmk"), check_vma=False
    )
```

```python
import functools

import jax
import jax.numpy as jnp
from jax import lax
from jax.experimental import pallas as pl
from jax.experimental.pallas import tpu as pltpu
from jax.sharding import PartitionSpec as P

AXES = ("lib", "lmk")
NZ, NY, NX, NC = 4, 4, 4, 2
TILE = 256
TIES = [5, 5, 5, 5, 5, 12, 9, 9, 9, 9, 9]
TAIL = 5 * 10**10
X1 = 4
X2 = 6
TV = 8 * 10**9


def pairs_of(move):
    pairs = []
    for z in range(NZ):
        for y in range(NY):
            for x in range(NX):
                for c in range(NC):
                    tz, ty, tx, tc = move(z, y, x, c, 1 if c == 0 else -1)
                    to = ((tz % NZ * NY + ty % NY) * NX + tx % NX) * NC + tc
                    pairs.append((((z * NY + y) * NX + x) * NC + c, to))
    return pairs


PAIRS = {
    "z": pairs_of(lambda z, y, x, c, s: (z + s, y, x, c)),
    "y": pairs_of(lambda z, y, x, c, s: (z, y + s, x, c)),
    "x": pairs_of(lambda z, y, x, c, s: (z, y, x + s, c)),
    "core": pairs_of(lambda z, y, x, c, s: (z, y, x, 1 - c)),
}


def send(block, axis):
    return lax.ppermute(block, AXES, PAIRS[axis])


def vmem(x):
    return pltpu.with_memory_space_constraint(x, pltpu.VMEM)


def hbm(x):
    return pltpu.with_memory_space_constraint(x, pltpu.HBM)


def position():
    lib, lmk = lax.axis_index("lib"), lax.axis_index("lmk")
    return lib // NY, lib % NY, lmk // NC, lmk % NC


def root_index(i, j):
    z, y, _, c = position()
    back = 3 + 2 * c
    return (z + i * back) % NZ * NY + (y + j * back) % NY


def kernel_index(i):
    _, _, x, c = position()
    return (x + i * (3 + 2 * c)) % NX * 4


VM = pl.BlockSpec(memory_space=pltpu.VMEM)
ANY = pl.BlockSpec(memory_space=pl.ANY)


def params(mib):
    return pltpu.CompilerParams(vmem_limit_bytes=mib * 2**20)


def cost(flops, bytes_accessed=0):
    return pl.CostEstimate(flops=flops, bytes_accessed=bytes_accessed, transcendentals=0)


def tversky_kernel(row_bits, row_scale, col_bits, got_bits, out, rbuf, cbuf, sems):
    core = position()[3]
    copies = [
        pltpu.make_async_copy(row_bits.at[pl.ds(t * TILE, TILE), :], rbuf.at[pl.ds(t * TILE, TILE), :], sems.at[t])
        for t in range(3)
    ] + [
        pltpu.make_async_copy(
            col_bits.at[pl.ds(pl.multiple_of(h * 512 + core * 256, 256), 256), :],
            cbuf.at[pl.ds(h * 256, 256), :],
            sems.at[3 + h],
        )
        for h in range(2)
    ]
    for at in (0, 3, 4, 1, 2):
        copies[at].start()
    copies[3].wait()
    copies[4].wait()
    ones = jnp.ones((8, row_bits.shape[1]), jnp.bfloat16)
    nt = (((1,), (1,)), ((), ()))
    for part, bits in enumerate((cbuf, got_bits)):
        count = lax.dot_general(ones, bits[...], nt, preferred_element_type=jnp.float32)[:1, :]
        col_scale = 0.1 * count
        first = 2 * (core if part == 0 else 1 - core)
        for t in range(3):
            if part == 0:
                copies[t].wait()
            rows = slice(t * TILE, (t + 1) * TILE)
            common = lax.dot_general(rbuf[rows, :], bits[...], nt, preferred_element_type=jnp.float32)
            k = (common / (row_scale[rows, :] + col_scale)).astype(jnp.bfloat16)
            for h in range(2):
                out[first + h, rows, :] = k[:, h * 256 : (h + 1) * 256]


def tversky(row_bits, row_count, col_bits, got_bits):
    row_scale = 0.9 * row_count.astype(jnp.float32)[:, None]
    rows = row_bits.shape[0]
    return pl.pallas_call(
        tversky_kernel,
        out_shape=pltpu.VMEM((4, rows, 256), jnp.bfloat16),
        in_specs=[ANY, VM, ANY, VM],
        out_specs=VM,
        scratch_shapes=[
            pltpu.VMEM(row_bits.shape, jnp.bfloat16),
            pltpu.VMEM((512, row_bits.shape[1]), jnp.bfloat16),
            pltpu.SemaphoreType.DMA((5,)),
        ],
        compiler_params=params(12),
        cost_estimate=cost(TV),
    )(hbm(row_bits), vmem(row_scale), hbm(col_bits), vmem(got_bits))


def tie_kernel(*refs):
    pass


def tie(*arrays, flops):
    return pl.pallas_call(
        tie_kernel,
        out_shape=tuple(pltpu.VMEM(a.shape, a.dtype) for a in arrays),
        in_specs=[VM] * len(arrays),
        out_specs=(VM,) * len(arrays),
        input_output_aliases={i: i for i in range(len(arrays))},
        compiler_params=params(1),
        cost_estimate=cost(flops),
    )(*map(vmem, arrays))


def place_kernel(hops, has_full, *refs):
    n = len(hops)
    blocks, full, sems = refs[:n], refs[n + has_full], refs[n + has_full + 1]
    copies = [
        pltpu.make_async_copy(b, full.at[pl.ds(kernel_index(i), 4)], sems.at[at])
        for at, (i, b) in enumerate(zip(hops, blocks))
    ]
    for cp in copies:
        cp.start()
    for cp in copies:
        cp.wait()


def place(hops, blocks, full=None):
    args = [*map(vmem, blocks)] + ([] if full is None else [vmem(full)])
    return pl.pallas_call(
        functools.partial(place_kernel, hops, full is not None),
        out_shape=pltpu.VMEM((16, *blocks[0].shape[1:]), blocks[0].dtype),
        in_specs=[VM] * len(args),
        out_specs=VM,
        scratch_shapes=[pltpu.SemaphoreType.DMA((len(hops),))],
        input_output_aliases={} if full is None else {len(hops): 0},
        compiler_params=params(1),
        cost_estimate=cost(10**6),
    )(*args)


def partial_kernel(terms, n_r, n_acc, hops, k, *refs):
    rs, accs, outs = refs[:n_r], refs[n_r : n_r + n_acc], refs[n_r + n_acc :]
    z, _, x, c = position()
    ahead = (x - z) * (1 - 2 * c) + 4

    def tile(t, carry):
        rows = pl.ds(t * TILE, TILE)
        for o, halves in enumerate(terms):
            if not n_acc:
                outs[o][rows, :] = jnp.zeros((TILE, 1024), jnp.float32)
            for i in range(4):
                hop = (ahead + i) % 4
                with_hop = (hop >= hops[0]) & (hop <= hops[-1])

                @pl.when(with_hop)
                def _():
                    for half, pieces in enumerate(halves):
                        cols = slice(half * 512, (half + 1) * 512)
                        total = outs[o][rows, cols]
                        for r, row0, col0, at in pieces:
                            if at[0] == i:
                                total += jnp.dot(
                                    k[root_index(*at), rows, :],
                                    rs[r][row0 : row0 + 256, col0 : col0 + 512],
                                    preferred_element_type=jnp.float32,
                                )
                        outs[o][rows, cols] = total

        return carry

    lax.fori_loop(0, outs[0].shape[0] // TILE, tile, 0)


def group_kernel(terms, n_r, n_acc, k, *refs):
    rs, accs, outs = refs[:n_r], refs[n_r : n_r + n_acc], refs[n_r + n_acc :]

    def tile(t, carry):
        rows = pl.ds(t * TILE, TILE)
        for o, halves in enumerate(terms):
            for half, pieces in enumerate(halves):
                cols = slice(half * 512, (half + 1) * 512)
                total = accs[o][rows, cols] if n_acc else None
                for r, row0, col0, at in pieces:
                    part = jnp.dot(
                        k[root_index(*at), rows, :],
                        rs[r][row0 : row0 + 256, col0 : col0 + 512],
                        preferred_element_type=jnp.float32,
                    )
                    total = part if total is None else total + part
                outs[o][rows, cols] = total
        return carry

    lax.fori_loop(0, outs[0].shape[0] // TILE, tile, 0)


def group(terms, rs, k, accs, hops=None):
    rows = k.shape[1]
    args = [*map(vmem, (k, *rs, *accs))]
    first = 1 + len(rs)
    return pl.pallas_call(
        functools.partial(group_kernel, terms, len(rs), len(accs))
        if hops is None
        else functools.partial(partial_kernel, terms, len(rs), len(accs), hops),
        out_shape=tuple(pltpu.VMEM((rows, 1024), jnp.float32) for _ in terms),
        in_specs=[VM] * len(args),
        out_specs=tuple(VM for _ in terms),
        input_output_aliases={first + i: i for i in range(len(accs))},
        compiler_params=params(8),
        cost_estimate=cost(10**6),
    )(*args)


def last_kernel(halves, n_r, k, *refs):
    rs, (acc, other, out, buf, sems) = refs[:n_r], refs[n_r:]
    copies = []
    for t in range(acc.shape[0] // TILE):
        rows = slice(t * TILE, (t + 1) * TILE)
        for half, pieces in enumerate(halves):
            cols = slice(half * 512, (half + 1) * 512)
            total = acc[rows, cols] + other[rows, cols]
            for r, row0, col0, at in pieces:
                total += jnp.dot(
                    k[root_index(*at), rows, :],
                    rs[r][row0 : row0 + 256, col0 : col0 + 512],
                    preferred_element_type=jnp.float32,
                )
            buf[rows, cols] = total
        cp = pltpu.make_async_copy(buf.at[pl.ds(t * TILE, TILE), :], out.at[pl.ds(t * TILE, TILE), :], sems.at[t])
        cp.start()
        copies.append(cp)
    for cp in copies:
        cp.wait()


def last(halves, rs, k, acc, other):
    rows = k.shape[1]
    args = [*map(vmem, (k, *rs, acc, other))]
    return pl.pallas_call(
        functools.partial(last_kernel, halves, len(rs)),
        out_shape=jax.ShapeDtypeStruct((rows, 1024), jnp.float32),
        in_specs=[VM] * len(args),
        out_specs=ANY,
        scratch_shapes=[pltpu.VMEM((rows, 1024), jnp.float32), pltpu.SemaphoreType.DMA((rows // TILE,))],
        compiler_params=params(8),
        cost_estimate=cost(10**6),
    )(*args)


def shards(library_bits, library_count, landmark_bits, landmark_count, inverse_root):
    core = lax.axis_index("lmk") % NC
    mine = lax.dynamic_slice_in_dim(inverse_root, core * 256, 256, 0)
    theirs = send(lax.dynamic_slice_in_dim(inverse_root, (1 - core) * 256, 256, 0), "core")
    blocks = landmark_bits.reshape(2, 512, -1)
    bits = send(lax.dynamic_slice_in_dim(blocks, (1 - core) * 256, 256, 1).reshape(512, -1), "core")
    own = [theirs, mine]
    first = [[[], []] for _ in range(2)]
    second = [[[], []] for _ in range(2)]
    for s in range(2):
        first[s][0].append(send(own[s], "y"))
        first[s][1].append(send(own[s], "z"))
    ks = [tversky(library_bits, library_count, landmark_bits, bits)]

    def second_terms(hop, p):
        return [[(p, 256 * m, 0, (hop, m + 1)) for m in range(3)], [(p + 1, 256 * m, 0, (m + 1, hop)) for m in range(3)]]

    accs = None
    for step in range(11):
        s, hop = step % 2, step // 2
        rings = (first if hop < 3 else second)[s]
        ready = [rings[0][hop % 3], rings[1][hop % 3]]
        if step == 8:
            k = place([0, 1, 2], ks[:3])
            rs, terms = [], []
            for o in range(2):
                p = len(rs)
                rs += [own[o], *first[o][0], *first[o][1], second[o][0][0], second[o][1][0]]
                where = [(0, 0), (0, 1), (0, 2), (0, 3), (1, 0), (2, 0), (3, 0)]
                more = second_terms(1, p + 7)
                terms.append([[(p + n, 0, 512 * h, at) for n, at in enumerate(where)] + more[h] for h in range(2)])
            accs = group(terms, rs, k, [], (0, 2))
        if step == 0:
            token = jnp.zeros((16, 128), jnp.bfloat16)
        if step in (X1, X2):
            tied = tie(token, *ready, ks[-1], flops=TIES[step] * 10**9)
            ks[-1] = tied[-1]
        else:
            tied = tie(token, *ready, flops=TIES[step] * 10**9)
        token = tied[0]
        rings[0][hop % 3], rings[1][hop % 3] = done = tied[1:3]
        if hop < 2:
            rings[0].append(send(done[0], "y"))
            rings[1].append(send(done[1], "z"))
        elif hop == 2:
            left = jnp.concatenate([q[:, :512] for q in rings[0]])
            right = jnp.concatenate([q[:, 512:] for q in rings[1]])
            second[s][0].append(send(left, "z"))
            second[s][1].append(send(right, "y"))
        elif hop < 5:
            rings[0].append(send(done[0], "z"))
            rings[1].append(send(done[1], "y"))
        if step in (0, X1, X2):
            ks.append(send(ks[-1], "x"))
    k = place([3], ks[3:], k)
    accs = group(terms, rs, k, accs, (3, 3))
    rs = [second[s][a][1] for s in range(2) for a in range(2)]
    accs = group([second_terms(2, 0), second_terms(2, 2)], rs, k, accs)
    (theirs,) = group([second_terms(3, 0)], [second[0][0][2], second[0][1][2]], k, accs[:1])
    other = send(theirs, "core")
    tail = tie(second[1][0][2], second[1][1][2], flops=TAIL)
    return last(second_terms(3, 0), tail, k, accs[1], other)


def solution(mesh):
    placed = (P("lib", None), P("lib"), P("lmk", None), P("lmk"), P("lib", "lmk"))
    return jax.shard_map(
        shards, mesh=mesh, in_specs=placed, out_specs=P("lib", "lmk"), check_vma=False
    )
```

```python
import functools

import jax
import jax.numpy as jnp
from jax import lax
from jax.experimental import pallas as pl
from jax.experimental.pallas import tpu as pltpu
from jax.sharding import PartitionSpec as P

AXES = ("lib", "lmk")
NZ, NY, NX, NC = 4, 4, 4, 2
TILE = 256
TIES = [5, 7, 7, 7, 7, 7, 9, 9, 9, 9, 9]
TAIL = 5 * 10**10
X1 = 3
X2 = 6
TV = 8 * 10**9


def pairs_of(move):
    pairs = []
    for z in range(NZ):
        for y in range(NY):
            for x in range(NX):
                for c in range(NC):
                    tz, ty, tx, tc = move(z, y, x, c, 1 if c == 0 else -1)
                    to = ((tz % NZ * NY + ty % NY) * NX + tx % NX) * NC + tc
                    pairs.append((((z * NY + y) * NX + x) * NC + c, to))
    return pairs


PAIRS = {
    "z": pairs_of(lambda z, y, x, c, s: (z + s, y, x, c)),
    "y": pairs_of(lambda z, y, x, c, s: (z, y + s, x, c)),
    "x": pairs_of(lambda z, y, x, c, s: (z, y, x + s, c)),
    "core": pairs_of(lambda z, y, x, c, s: (z, y, x, 1 - c)),
}


def send(block, axis):
    return lax.ppermute(block, AXES, PAIRS[axis])


def vmem(x):
    return pltpu.with_memory_space_constraint(x, pltpu.VMEM)


def hbm(x):
    return pltpu.with_memory_space_constraint(x, pltpu.HBM)


def position():
    lib, lmk = lax.axis_index("lib"), lax.axis_index("lmk")
    return lib // NY, lib % NY, lmk // NC, lmk % NC


def root_index(i, j):
    z, y, _, c = position()
    back = 3 + 2 * c
    return (z + i * back) % NZ * NY + (y + j * back) % NY


def kernel_index(i):
    _, _, x, c = position()
    return (x + i * (3 + 2 * c)) % NX * 4


VM = pl.BlockSpec(memory_space=pltpu.VMEM)
ANY = pl.BlockSpec(memory_space=pl.ANY)


def params(mib):
    return pltpu.CompilerParams(vmem_limit_bytes=mib * 2**20)


def cost(flops, bytes_accessed=0):
    return pl.CostEstimate(flops=flops, bytes_accessed=bytes_accessed, transcendentals=0)


def load_kernel(row_bits, col_bits, rbuf, cbuf, token, sems):
    core = position()[3]
    copies = [pltpu.make_async_copy(row_bits, rbuf, sems.at[0])] + [
        pltpu.make_async_copy(
            col_bits.at[pl.ds(pl.multiple_of(h * 512 + core * 256, 256), 256), :],
            cbuf.at[pl.ds(h * 256, 256), :],
            sems.at[1 + h],
        )
        for h in range(2)
    ]
    for cp in copies:
        cp.start()
    token[...] = jnp.zeros(token.shape, token.dtype)
    for cp in copies:
        cp.wait()


def load(row_bits, col_bits):
    rows, depth = row_bits.shape
    return pl.pallas_call(
        load_kernel,
        out_shape=(
            pltpu.VMEM((rows, depth), jnp.bfloat16),
            pltpu.VMEM((512, depth), jnp.bfloat16),
            pltpu.VMEM((16, 128), jnp.bfloat16),
        ),
        in_specs=[ANY, ANY],
        out_specs=(VM,) * 3,
        scratch_shapes=[pltpu.SemaphoreType.DMA((3,))],
        compiler_params=params(1),
        cost_estimate=cost(10**6),
    )(hbm(row_bits), hbm(col_bits))


def tversky_kernel(row_bits, row_scale, col_bits, col_scale, got_bits, out, gbuf, ones, sems):
    core = position()[3]
    nt = (((1,), (1,)), ((), ()))
    cols = [pl.multiple_of(h * 512 + core * 256, 256) for h in range(2)]
    copies = [
        pltpu.make_async_copy(got_bits.at[pl.ds(cols[h], 256), :], gbuf.at[pl.ds(h * 256, 256), :], sems.at[h])
        for h in range(2)
    ]
    for cp in copies:
        cp.start()
    ones[...] = jnp.ones(ones.shape, ones.dtype)
    for part, bits_ref in enumerate((col_bits, gbuf)):
        for h in range(2):
            if part == 1:
                copies[h].wait()
            bits = bits_ref[h * 256 : (h + 1) * 256, :]
            if part == 0:
                scale, to = col_scale[:, pl.ds(cols[h], 256)], 2 * core + h
            else:
                count = lax.dot_general(ones[...], bits, nt, preferred_element_type=jnp.float32)[:1, :]
                scale, to = 0.1 * count, 2 * (1 - core) + h
            for t in range(row_bits.shape[0] // TILE):
                rows = slice(t * TILE, (t + 1) * TILE)
                common = lax.dot_general(row_bits[rows, :], bits, nt, preferred_element_type=jnp.float32)
                out[to, rows, :] = (common / (row_scale[rows, :] + scale)).astype(jnp.bfloat16)


def tversky(row_bits, row_scale, col_bits, col_scale, got_bits):
    rows, depth = row_bits.shape
    return pl.pallas_call(
        tversky_kernel,
        out_shape=pltpu.VMEM((4, rows, 256), jnp.bfloat16),
        in_specs=[VM, VM, VM, VM, ANY],
        out_specs=VM,
        scratch_shapes=[
            pltpu.VMEM((512, depth), jnp.bfloat16),
            pltpu.VMEM((TILE, depth), jnp.bfloat16),
            pltpu.SemaphoreType.DMA((2,)),
        ],
        compiler_params=params(8),
        cost_estimate=cost(TV),
    )(*map(vmem, (row_bits, row_scale, col_bits, col_scale, got_bits)))


def tie_kernel(*refs):
    pass


def tie(*arrays, flops):
    return pl.pallas_call(
        tie_kernel,
        out_shape=tuple(pltpu.VMEM(a.shape, a.dtype) for a in arrays),
        in_specs=[VM] * len(arrays),
        out_specs=(VM,) * len(arrays),
        input_output_aliases={i: i for i in range(len(arrays))},
        compiler_params=params(1),
        cost_estimate=cost(flops),
    )(*map(vmem, arrays))


def place_kernel(hops, has_full, *refs):
    n = len(hops)
    blocks, full, sems = refs[:n], refs[n + has_full], refs[n + has_full + 1]
    copies = [
        pltpu.make_async_copy(b, full.at[pl.ds(kernel_index(i), 4)], sems.at[at])
        for at, (i, b) in enumerate(zip(hops, blocks))
    ]
    for cp in copies:
        cp.start()
    for cp in copies:
        cp.wait()


def place(hops, blocks, full=None):
    args = [*map(vmem, blocks)] + ([] if full is None else [vmem(full)])
    return pl.pallas_call(
        functools.partial(place_kernel, hops, full is not None),
        out_shape=pltpu.VMEM((16, *blocks[0].shape[1:]), blocks[0].dtype),
        in_specs=[VM] * len(args),
        out_specs=VM,
        scratch_shapes=[pltpu.SemaphoreType.DMA((len(hops),))],
        input_output_aliases={} if full is None else {len(hops): 0},
        compiler_params=params(1),
        cost_estimate=cost(10**6),
    )(*args)


def sum_kernel(jobs, n_r, n_acc, k, *refs):
    rs, accs, outs = refs[:n_r], refs[n_r : n_r + n_acc], refs[n_r + n_acc :]
    z, _, x, c = position()
    ahead = (x - z) * (1 - 2 * c) + 4

    def tile(t, carry):
        rows = pl.ds(t * TILE, TILE)

        def add(out, half, pieces, start):
            cols = slice(half * 512, (half + 1) * 512)
            total = start[rows, cols]
            for r, row0, col0, at in pieces:
                total += jnp.dot(
                    k[root_index(*at), rows, :],
                    rs[r][row0 : row0 + 256, col0 : col0 + 512],
                    preferred_element_type=jnp.float32,
                )
            out[rows, cols] = total

        for out, (acc, hops, terms) in zip(outs, jobs):
            if hops is None:
                for half, pieces in enumerate(terms):
                    add(out, half, pieces, accs[acc])
                continue
            if acc is None:
                out[rows, :] = jnp.zeros((TILE, 1024), jnp.float32)
            for i in range(4):
                hop = (ahead + i) % 4

                @pl.when((hop >= hops[0]) & (hop <= hops[1]))
                def _():
                    for half, pieces in enumerate(terms):
                        here = [p for p in pieces if p[3][0] == i]
                        if here:
                            add(out, half, here, out)

        return carry

    lax.fori_loop(0, outs[0].shape[0] // TILE, tile, 0)


def sums(jobs, rs, k, accs):
    rows = k.shape[1]
    args = [*map(vmem, (k, *rs, *accs))]
    first = 1 + len(rs)
    return pl.pallas_call(
        functools.partial(sum_kernel, jobs, len(rs), len(accs)),
        out_shape=tuple(pltpu.VMEM((rows, 1024), jnp.float32) for _ in jobs),
        in_specs=[VM] * len(args),
        out_specs=tuple(VM for _ in jobs),
        input_output_aliases={first + acc: o for o, (acc, _, _) in enumerate(jobs) if acc is not None},
        compiler_params=params(8),
        cost_estimate=cost(10**6),
    )(*args)


def last_kernel(halves, n_r, k, *refs):
    rs, (acc, other, out, buf, sems) = refs[:n_r], refs[n_r:]
    copies = []
    for t in range(acc.shape[0] // TILE):
        rows = slice(t * TILE, (t + 1) * TILE)
        for half, pieces in enumerate(halves):
            cols = slice(half * 512, (half + 1) * 512)
            total = acc[rows, cols] + other[rows, cols]
            for r, row0, col0, at in pieces:
                total += jnp.dot(
                    k[root_index(*at), rows, :],
                    rs[r][row0 : row0 + 256, col0 : col0 + 512],
                    preferred_element_type=jnp.float32,
                )
            buf[rows, cols] = total
        cp = pltpu.make_async_copy(buf.at[pl.ds(t * TILE, TILE), :], out.at[pl.ds(t * TILE, TILE), :], sems.at[t])
        cp.start()
        copies.append(cp)
    for cp in copies:
        cp.wait()


def last(halves, rs, k, acc, other):
    rows = k.shape[1]
    args = [*map(vmem, (k, *rs, acc, other))]
    return pl.pallas_call(
        functools.partial(last_kernel, halves, len(rs)),
        out_shape=jax.ShapeDtypeStruct((rows, 1024), jnp.float32),
        in_specs=[VM] * len(args),
        out_specs=ANY,
        scratch_shapes=[pltpu.VMEM((rows, 1024), jnp.float32), pltpu.SemaphoreType.DMA((rows // TILE,))],
        compiler_params=params(8),
        cost_estimate=cost(10**6),
    )(*args)


def shards(library_bits, library_count, landmark_bits, landmark_count, inverse_root):
    core = lax.axis_index("lmk") % NC
    mine = lax.dynamic_slice_in_dim(inverse_root, core * 256, 256, 0)
    theirs = send(lax.dynamic_slice_in_dim(inverse_root, (1 - core) * 256, 256, 0), "core")
    row_scale = 0.9 * library_count.astype(jnp.float32)[:, None]
    col_scale = 0.1 * landmark_count.astype(jnp.float32)[None, :]
    row_bits, col_bits, token = load(library_bits, landmark_bits)
    theirs, token = tie(theirs, token, flops=10**6)
    own = [theirs, mine]
    first = [[[], []] for _ in range(2)]
    second = [[[], []] for _ in range(2)]
    for s in range(2):
        first[s][0].append(send(own[s], "y"))
        first[s][1].append(send(own[s], "z"))
    ks = [tversky(row_bits, row_scale, col_bits, col_scale, send(landmark_bits, "core"))]

    def second_terms(hop, p):
        return [[(p, 256 * m, 0, (hop, m + 1)) for m in range(3)], [(p + 1, 256 * m, 0, (m + 1, hop)) for m in range(3)]]

    def first_terms(s, p):
        rs = [own[s], *first[s][0], *first[s][1], second[s][0][0], second[s][1][0]]
        where = [(0, 0), (0, 1), (0, 2), (0, 3), (1, 0), (2, 0), (3, 0)]
        more = second_terms(1, p + 7)
        return [[(p + n, 0, 512 * h, at) for n, at in enumerate(where)] + more[h] for h in range(2)], rs

    for step in range(10):
        s, hop = step % 2, step // 2
        rings = (first if hop < 3 else second)[s]
        ready = [rings[0][hop % 3], rings[1][hop % 3]]
        if step == 8:
            k = place([0, 1, 2], ks[:3])
            terms, rs = first_terms(0, 0)
            (acc,) = sums([(None, (0, 2), terms)], rs, k, [])
            ready.append(acc)
        if step == 9:
            terms, rs = first_terms(1, 0)
            jobs = [(None, (0, 2), terms), (0, (0, 2), second_terms(2, len(rs)))]
            other, acc = sums(jobs, [*rs, second[0][0][1], second[0][1][1]], k, [acc])
            ready.append(other)
        if step in (X1, X2):
            ready.append(ks[-1])
        token, *done = tie(token, *ready, flops=TIES[step] * 10**9)
        rings[0][hop % 3], rings[1][hop % 3] = done[:2]
        if step == 8:
            acc = done[2]
        if step == 9:
            other = done[2]
        if step in (X1, X2):
            ks[-1] = done[2]
        if hop < 2:
            rings[0].append(send(done[0], "y"))
            rings[1].append(send(done[1], "z"))
        elif hop == 2:
            left = jnp.concatenate([q[:, :512] for q in rings[0]])
            right = jnp.concatenate([q[:, 512:] for q in rings[1]])
            second[s][0].append(send(left, "z"))
            second[s][1].append(send(right, "y"))
        elif hop < 5:
            rings[0].append(send(done[0], "z"))
            rings[1].append(send(done[1], "y"))
        if step in (0, X1, X2):
            ks.append(send(ks[-1], "x"))

    k = place([3], ks[3:], k)
    terms, rs = first_terms(0, 0)
    more = second_terms(2, len(rs))
    terms = [terms[h] + more[h] for h in range(2)]
    (acc,) = sums([(0, (3, 3), terms)], [*rs, second[0][0][1], second[0][1][1]], k, [acc])
    (acc,) = sums([(0, None, second_terms(3, 0))], [second[0][0][2], second[0][1][2]], k, [acc])
    theirs = send(acc, "core")
    terms, rs = first_terms(1, 0)
    (other,) = sums([(0, (3, 3), terms)], rs, k, [other])
    (other,) = sums([(0, None, second_terms(2, 0))], [second[1][0][1], second[1][1][1]], k, [other])
    tail = tie(second[1][0][2], second[1][1][2], flops=TAIL)
    return last(second_terms(3, 0), tail, k, other, theirs)


def solution(mesh):
    placed = (P("lib", None), P("lib"), P("lmk", None), P("lmk"), P("lib", "lmk"))
    return jax.shard_map(
        shards, mesh=mesh, in_specs=placed, out_specs=P("lib", "lmk"), check_vma=False
    )
```

```python
import functools

import jax
import jax.numpy as jnp
from jax import lax
from jax.experimental import pallas as pl
from jax.experimental.pallas import tpu as pltpu
from jax.sharding import PartitionSpec as P

AXES = ("lib", "lmk")
NZ, NY, NX, NC = 4, 4, 4, 2
TILE = 256
TIES = [5, 7, 7, 7, 7, 5, 5, 5, 9, 9, 9]
TAIL = 5 * 10**10
X1 = 3
X2 = 7
TV = 8 * 10**9


def pairs_of(move):
    pairs = []
    for z in range(NZ):
        for y in range(NY):
            for x in range(NX):
                for c in range(NC):
                    tz, ty, tx, tc = move(z, y, x, c, 1 if c == 0 else -1)
                    to = ((tz % NZ * NY + ty % NY) * NX + tx % NX) * NC + tc
                    pairs.append((((z * NY + y) * NX + x) * NC + c, to))
    return pairs


PAIRS = {
    "z": pairs_of(lambda z, y, x, c, s: (z + s, y, x, c)),
    "y": pairs_of(lambda z, y, x, c, s: (z, y + s, x, c)),
    "x": pairs_of(lambda z, y, x, c, s: (z, y, x + s, c)),
    "core": pairs_of(lambda z, y, x, c, s: (z, y, x, 1 - c)),
}


def send(block, axis):
    return lax.ppermute(block, AXES, PAIRS[axis])


def vmem(x):
    return pltpu.with_memory_space_constraint(x, pltpu.VMEM)


def hbm(x):
    return pltpu.with_memory_space_constraint(x, pltpu.HBM)


def position():
    lib, lmk = lax.axis_index("lib"), lax.axis_index("lmk")
    return lib // NY, lib % NY, lmk // NC, lmk % NC


def root_index(i, j):
    z, y, _, c = position()
    back = 3 + 2 * c
    return (z + i * back) % NZ * NY + (y + j * back) % NY


def kernel_index(i):
    _, _, x, c = position()
    return (x + i * (3 + 2 * c)) % NX * 4


VM = pl.BlockSpec(memory_space=pltpu.VMEM)
ANY = pl.BlockSpec(memory_space=pl.ANY)


def params(mib):
    return pltpu.CompilerParams(vmem_limit_bytes=mib * 2**20)


def cost(flops, bytes_accessed=0):
    return pl.CostEstimate(flops=flops, bytes_accessed=bytes_accessed, transcendentals=0)


def load_kernel(row_bits, col_bits, rbuf, cbuf, token, sems):
    core = position()[3]
    copies = [pltpu.make_async_copy(row_bits, rbuf, sems.at[0])] + [
        pltpu.make_async_copy(
            col_bits.at[pl.ds(pl.multiple_of(h * 512 + core * 256, 256), 256), :],
            cbuf.at[pl.ds(h * 256, 256), :],
            sems.at[1 + h],
        )
        for h in range(2)
    ]
    for cp in copies:
        cp.start()
    token[...] = jnp.zeros(token.shape, token.dtype)
    for cp in copies:
        cp.wait()


def load(row_bits, col_bits):
    rows, depth = row_bits.shape
    return pl.pallas_call(
        load_kernel,
        out_shape=(
            pltpu.VMEM((rows, depth), jnp.bfloat16),
            pltpu.VMEM((512, depth), jnp.bfloat16),
            pltpu.VMEM((16, 128), jnp.bfloat16),
        ),
        in_specs=[ANY, ANY],
        out_specs=(VM,) * 3,
        scratch_shapes=[pltpu.SemaphoreType.DMA((3,))],
        compiler_params=params(1),
        cost_estimate=cost(10**6),
    )(hbm(row_bits), hbm(col_bits))


def tversky_kernel(row_bits, row_scale, col_bits, col_scale, got_bits, out, gbuf, ones, sems):
    core = position()[3]
    nt = (((1,), (1,)), ((), ()))
    cols = [pl.multiple_of(h * 512 + core * 256, 256) for h in range(2)]
    copies = [
        pltpu.make_async_copy(got_bits.at[pl.ds(cols[h], 256), :], gbuf.at[pl.ds(h * 256, 256), :], sems.at[h])
        for h in range(2)
    ]
    for cp in copies:
        cp.start()
    ones[...] = jnp.ones(ones.shape, ones.dtype)
    for part, bits_ref in enumerate((col_bits, gbuf)):
        for h in range(2):
            if part == 1:
                copies[h].wait()
            bits = bits_ref[h * 256 : (h + 1) * 256, :]
            if part == 0:
                scale, to = col_scale[:, pl.ds(cols[h], 256)], 2 * core + h
            else:
                count = lax.dot_general(ones[...], bits, nt, preferred_element_type=jnp.float32)[:1, :]
                scale, to = 0.1 * count, 2 * (1 - core) + h
            for t in range(row_bits.shape[0] // TILE):
                rows = slice(t * TILE, (t + 1) * TILE)
                common = lax.dot_general(row_bits[rows, :], bits, nt, preferred_element_type=jnp.float32)
                out[to, rows, :] = (common / (row_scale[rows, :] + scale)).astype(jnp.bfloat16)


def tversky(row_bits, row_scale, col_bits, col_scale, got_bits):
    rows, depth = row_bits.shape
    return pl.pallas_call(
        tversky_kernel,
        out_shape=pltpu.VMEM((4, rows, 256), jnp.bfloat16),
        in_specs=[VM, VM, VM, VM, ANY],
        out_specs=VM,
        scratch_shapes=[
            pltpu.VMEM((512, depth), jnp.bfloat16),
            pltpu.VMEM((TILE, depth), jnp.bfloat16),
            pltpu.SemaphoreType.DMA((2,)),
        ],
        compiler_params=params(8),
        cost_estimate=cost(TV),
    )(*map(vmem, (row_bits, row_scale, col_bits, col_scale, got_bits)))


def tie_kernel(*refs):
    pass


def tie(*arrays, flops):
    return pl.pallas_call(
        tie_kernel,
        out_shape=tuple(pltpu.VMEM(a.shape, a.dtype) for a in arrays),
        in_specs=[VM] * len(arrays),
        out_specs=(VM,) * len(arrays),
        input_output_aliases={i: i for i in range(len(arrays))},
        compiler_params=params(1),
        cost_estimate=cost(flops),
    )(*map(vmem, arrays))


def place_kernel(hops, has_full, *refs):
    n = len(hops)
    blocks, full, sems = refs[:n], refs[n + has_full], refs[n + has_full + 1]
    copies = [
        pltpu.make_async_copy(b, full.at[pl.ds(kernel_index(i), 4)], sems.at[at])
        for at, (i, b) in enumerate(zip(hops, blocks))
    ]
    for cp in copies:
        cp.start()
    for cp in copies:
        cp.wait()


def place(hops, blocks, full=None):
    args = [*map(vmem, blocks)] + ([] if full is None else [vmem(full)])
    return pl.pallas_call(
        functools.partial(place_kernel, hops, full is not None),
        out_shape=pltpu.VMEM((16, *blocks[0].shape[1:]), blocks[0].dtype),
        in_specs=[VM] * len(args),
        out_specs=VM,
        scratch_shapes=[pltpu.SemaphoreType.DMA((len(hops),))],
        input_output_aliases={} if full is None else {len(hops): 0},
        compiler_params=params(1),
        cost_estimate=cost(10**6),
    )(*args)


def sum_kernel(jobs, n_r, n_acc, k, *refs):
    rs, accs, outs = refs[:n_r], refs[n_r : n_r + n_acc], refs[n_r + n_acc :]
    z, _, x, c = position()
    ahead = (x - z) * (1 - 2 * c) + 4

    def tile(t, carry):
        rows = pl.ds(t * TILE, TILE)

        def add(out, half, pieces, start):
            cols = slice(half * 512, (half + 1) * 512)
            total = start[rows, cols]
            for r, row0, col0, at in pieces:
                total += jnp.dot(
                    k[root_index(*at), rows, :],
                    rs[r][row0 : row0 + 256, col0 : col0 + 512],
                    preferred_element_type=jnp.float32,
                )
            out[rows, cols] = total

        for out, (acc, hops, terms) in zip(outs, jobs):
            if hops is None:
                for half, pieces in enumerate(terms):
                    add(out, half, pieces, accs[acc])
                continue
            if acc is None:
                out[rows, :] = jnp.zeros((TILE, 1024), jnp.float32)
            for i in range(4):
                hop = (ahead + i) % 4

                @pl.when((hop >= hops[0]) & (hop <= hops[1]))
                def _():
                    for half, pieces in enumerate(terms):
                        here = [p for p in pieces if p[3][0] == i]
                        if here:
                            add(out, half, here, out)

        return carry

    lax.fori_loop(0, outs[0].shape[0] // TILE, tile, 0)


def sums(jobs, rs, k, accs):
    rows = k.shape[1]
    args = [*map(vmem, (k, *rs, *accs))]
    first = 1 + len(rs)
    return pl.pallas_call(
        functools.partial(sum_kernel, jobs, len(rs), len(accs)),
        out_shape=tuple(pltpu.VMEM((rows, 1024), jnp.float32) for _ in jobs),
        in_specs=[VM] * len(args),
        out_specs=tuple(VM for _ in jobs),
        input_output_aliases={first + acc: o for o, (acc, _, _) in enumerate(jobs) if acc is not None},
        compiler_params=params(8),
        cost_estimate=cost(10**6),
    )(*args)


def last_kernel(halves, n_r, k, *refs):
    rs, (acc, other, out, buf, sems) = refs[:n_r], refs[n_r:]
    copies = []
    for t in range(acc.shape[0] // TILE):
        rows = slice(t * TILE, (t + 1) * TILE)
        for half, pieces in enumerate(halves):
            cols = slice(half * 512, (half + 1) * 512)
            total = acc[rows, cols] + other[rows, cols]
            for r, row0, col0, at in pieces:
                total += jnp.dot(
                    k[root_index(*at), rows, :],
                    rs[r][row0 : row0 + 256, col0 : col0 + 512],
                    preferred_element_type=jnp.float32,
                )
            buf[rows, cols] = total
        cp = pltpu.make_async_copy(buf.at[pl.ds(t * TILE, TILE), :], out.at[pl.ds(t * TILE, TILE), :], sems.at[t])
        cp.start()
        copies.append(cp)
    for cp in copies:
        cp.wait()


def last(halves, rs, k, acc, other):
    rows = k.shape[1]
    args = [*map(vmem, (k, *rs, acc, other))]
    return pl.pallas_call(
        functools.partial(last_kernel, halves, len(rs)),
        out_shape=jax.ShapeDtypeStruct((rows, 1024), jnp.float32),
        in_specs=[VM] * len(args),
        out_specs=ANY,
        scratch_shapes=[pltpu.VMEM((rows, 1024), jnp.float32), pltpu.SemaphoreType.DMA((rows // TILE,))],
        compiler_params=params(8),
        cost_estimate=cost(10**6),
    )(*args)


def shards(library_bits, library_count, landmark_bits, landmark_count, inverse_root):
    core = lax.axis_index("lmk") % NC
    mine = lax.dynamic_slice_in_dim(inverse_root, core * 256, 256, 0)
    theirs = send(lax.dynamic_slice_in_dim(inverse_root, (1 - core) * 256, 256, 0), "core")
    row_scale = 0.9 * library_count.astype(jnp.float32)[:, None]
    col_scale = 0.1 * landmark_count.astype(jnp.float32)[None, :]
    row_bits, col_bits, token = load(library_bits, landmark_bits)
    theirs, token = tie(theirs, token, flops=10**6)
    own = [theirs, mine]
    first = [[[], []] for _ in range(2)]
    second = [[[], []] for _ in range(2)]
    for s in range(2):
        first[s][0].append(send(own[s], "y"))
        first[s][1].append(send(own[s], "z"))
    ks = [tversky(row_bits, row_scale, col_bits, col_scale, send(landmark_bits, "core"))]

    def second_terms(hop, p):
        return [[(p, 256 * m, 0, (hop, m + 1)) for m in range(3)], [(p + 1, 256 * m, 0, (m + 1, hop)) for m in range(3)]]

    def first_terms(s, p):
        rs = [own[s], *first[s][0], *first[s][1], second[s][0][0], second[s][1][0]]
        where = [(0, 0), (0, 1), (0, 2), (0, 3), (1, 0), (2, 0), (3, 0)]
        more = second_terms(1, p + 7)
        return [[(p + n, 0, 512 * h, at) for n, at in enumerate(where)] + more[h] for h in range(2)], rs

    for step in range(10):
        s, hop = step % 2, step // 2
        rings = (first if hop < 3 else second)[s]
        ready = [rings[0][hop % 3], rings[1][hop % 3]]
        if step == 8:
            k = place([0, 1, 2], ks[:3])
            terms, rs = first_terms(0, 0)
            (acc,) = sums([(None, (0, 2), terms)], rs, k, [])
            ready.append(acc)
        if step == 9:
            terms, rs = first_terms(1, 0)
            jobs = [(None, (0, 2), terms), (0, (0, 2), second_terms(2, len(rs)))]
            other, acc = sums(jobs, [*rs, second[0][0][1], second[0][1][1]], k, [acc])
            ready.append(other)
        if step in (X1, X2):
            ready.append(ks[-1])
        token, *done = tie(token, *ready, flops=TIES[step] * 10**9)
        rings[0][hop % 3], rings[1][hop % 3] = done[:2]
        if step == 8:
            acc = done[2]
        if step == 9:
            other = done[2]
        if step in (X1, X2):
            ks[-1] = done[2]
        if hop < 2:
            rings[0].append(send(done[0], "y"))
            rings[1].append(send(done[1], "z"))
        elif hop == 2:
            left = jnp.concatenate([q[:, :512] for q in rings[0]])
            right = jnp.concatenate([q[:, 512:] for q in rings[1]])
            second[s][0].append(send(left, "z"))
            second[s][1].append(send(right, "y"))
        elif hop < 5:
            rings[0].append(send(done[0], "z"))
            rings[1].append(send(done[1], "y"))
        if step in (0, X1, X2):
            ks.append(send(ks[-1], "x"))

    k = place([3], ks[3:], k)
    terms, rs = first_terms(0, 0)
    more = second_terms(2, len(rs))
    terms = [terms[h] + more[h] for h in range(2)]
    (acc,) = sums([(0, (3, 3), terms)], [*rs, second[0][0][1], second[0][1][1]], k, [acc])
    (acc,) = sums([(0, None, second_terms(3, 0))], [second[0][0][2], second[0][1][2]], k, [acc])
    theirs = send(acc, "core")
    terms, rs = first_terms(1, 0)
    (other,) = sums([(0, (3, 3), terms)], rs, k, [other])
    (other,) = sums([(0, None, second_terms(2, 0))], [second[1][0][1], second[1][1][1]], k, [other])
    tail = tie(second[1][0][2], second[1][1][2], flops=TAIL)
    return last(second_terms(3, 0), tail, k, other, theirs)


def solution(mesh):
    placed = (P("lib", None), P("lib"), P("lmk", None), P("lmk"), P("lib", "lmk"))
    return jax.shard_map(
        shards, mesh=mesh, in_specs=placed, out_specs=P("lib", "lmk"), check_vma=False
    )
```

```python
import functools

import jax
import jax.numpy as jnp
from jax import lax
from jax.experimental import pallas as pl
from jax.experimental.pallas import tpu as pltpu
from jax.sharding import PartitionSpec as P

AXES = ("lib", "lmk")
NZ, NY, NX, NC = 4, 4, 4, 2
TILE = 256
TIES = [5, 5, 5, 5, 5, 5, 5, 5, 9, 9, 9]
TAIL = 5 * 10**10
X1 = 4
X2 = 7
TV = 10**6
LD = 10**6


def pairs_of(move):
    pairs = []
    for z in range(NZ):
        for y in range(NY):
            for x in range(NX):
                for c in range(NC):
                    tz, ty, tx, tc = move(z, y, x, c, 1 if c == 0 else -1)
                    to = ((tz % NZ * NY + ty % NY) * NX + tx % NX) * NC + tc
                    pairs.append((((z * NY + y) * NX + x) * NC + c, to))
    return pairs


PAIRS = {
    "z": pairs_of(lambda z, y, x, c, s: (z + s, y, x, c)),
    "y": pairs_of(lambda z, y, x, c, s: (z, y + s, x, c)),
    "x": pairs_of(lambda z, y, x, c, s: (z, y, x + s, c)),
    "core": pairs_of(lambda z, y, x, c, s: (z, y, x, 1 - c)),
}


def send(block, axis):
    return lax.ppermute(block, AXES, PAIRS[axis])


def vmem(x):
    return pltpu.with_memory_space_constraint(x, pltpu.VMEM)


def hbm(x):
    return pltpu.with_memory_space_constraint(x, pltpu.HBM)


def position():
    lib, lmk = lax.axis_index("lib"), lax.axis_index("lmk")
    return lib // NY, lib % NY, lmk // NC, lmk % NC


def root_index(i, j):
    z, y, _, c = position()
    back = 3 + 2 * c
    return (z + i * back) % NZ * NY + (y + j * back) % NY


def kernel_index(i):
    _, _, x, c = position()
    return (x + i * (3 + 2 * c)) % NX * 4


VM = pl.BlockSpec(memory_space=pltpu.VMEM)
ANY = pl.BlockSpec(memory_space=pl.ANY)


def params(mib):
    return pltpu.CompilerParams(vmem_limit_bytes=mib * 2**20)


def cost(flops, bytes_accessed=0):
    return pl.CostEstimate(flops=flops, bytes_accessed=bytes_accessed, transcendentals=0)


def load_kernel(row_bits, col_bits, rbuf, cbuf, token, sems):
    core = position()[3]
    copies = [pltpu.make_async_copy(row_bits, rbuf, sems.at[0])] + [
        pltpu.make_async_copy(
            col_bits.at[pl.ds(pl.multiple_of(h * 512 + core * 256, 256), 256), :],
            cbuf.at[pl.ds(h * 256, 256), :],
            sems.at[1 + h],
        )
        for h in range(2)
    ]
    for cp in copies:
        cp.start()
    token[...] = jnp.zeros(token.shape, token.dtype)
    for cp in copies:
        cp.wait()


def load(row_bits, col_bits):
    rows, depth = row_bits.shape
    return pl.pallas_call(
        load_kernel,
        out_shape=(
            pltpu.VMEM((rows, depth), jnp.bfloat16),
            pltpu.VMEM((512, depth), jnp.bfloat16),
            pltpu.VMEM((16, 128), jnp.bfloat16),
        ),
        in_specs=[ANY, ANY],
        out_specs=(VM,) * 3,
        scratch_shapes=[pltpu.SemaphoreType.DMA((3,))],
        compiler_params=params(1),
        cost_estimate=cost(LD),
    )(hbm(row_bits), hbm(col_bits))


def pick_kernel(col_bits, out, sems):
    core = position()[3]
    copies = [
        pltpu.make_async_copy(
            col_bits.at[pl.ds(pl.multiple_of(h * 512 + (1 - core) * 256, 256), 256), :],
            out.at[pl.ds(h * 256, 256), :],
            sems.at[h],
        )
        for h in range(2)
    ]
    for cp in copies:
        cp.start()
    for cp in copies:
        cp.wait()


def pick(col_bits):
    return pl.pallas_call(
        pick_kernel,
        out_shape=pltpu.VMEM((512, col_bits.shape[1]), col_bits.dtype),
        in_specs=[ANY],
        out_specs=VM,
        scratch_shapes=[pltpu.SemaphoreType.DMA((2,))],
        compiler_params=params(1),
        cost_estimate=cost(10**6),
    )(hbm(col_bits))


def tversky_kernel(row_bits, row_scale, col_bits, col_scale, got_bits, out, ones):
    core = position()[3]
    nt = (((1,), (1,)), ((), ()))
    ones[...] = jnp.ones(ones.shape, ones.dtype)
    for part, bits_ref in enumerate((col_bits, got_bits)):
        for h in range(2):
            bits = bits_ref[h * 256 : (h + 1) * 256, :]
            if part == 0:
                scale, to = col_scale[:, pl.ds(pl.multiple_of(h * 512 + core * 256, 256), 256)], 2 * core + h
            else:
                count = lax.dot_general(ones[...], bits, nt, preferred_element_type=jnp.float32)[:1, :]
                scale, to = 0.1 * count, 2 * (1 - core) + h
            for t in range(row_bits.shape[0] // TILE):
                rows = slice(t * TILE, (t + 1) * TILE)
                common = lax.dot_general(row_bits[rows, :], bits, nt, preferred_element_type=jnp.float32)
                out[to, rows, :] = (common / (row_scale[rows, :] + scale)).astype(jnp.bfloat16)


def tversky(row_bits, row_scale, col_bits, col_scale, got_bits):
    rows, depth = row_bits.shape
    return pl.pallas_call(
        tversky_kernel,
        out_shape=pltpu.VMEM((4, rows, 256), jnp.bfloat16),
        in_specs=[VM] * 5,
        out_specs=VM,
        scratch_shapes=[pltpu.VMEM((TILE, depth), jnp.bfloat16)],
        compiler_params=params(8),
        cost_estimate=cost(TV),
    )(*map(vmem, (row_bits, row_scale, col_bits, col_scale, got_bits)))


def tie_kernel(*refs):
    pass


def tie(*arrays, flops):
    return pl.pallas_call(
        tie_kernel,
        out_shape=tuple(pltpu.VMEM(a.shape, a.dtype) for a in arrays),
        in_specs=[VM] * len(arrays),
        out_specs=(VM,) * len(arrays),
        input_output_aliases={i: i for i in range(len(arrays))},
        compiler_params=params(1),
        cost_estimate=cost(flops),
    )(*map(vmem, arrays))


def place_kernel(hops, has_full, *refs):
    n = len(hops)
    blocks, full, sems = refs[:n], refs[n + has_full], refs[n + has_full + 1]
    copies = [
        pltpu.make_async_copy(b, full.at[pl.ds(kernel_index(i), 4)], sems.at[at])
        for at, (i, b) in enumerate(zip(hops, blocks))
    ]
    for cp in copies:
        cp.start()
    for cp in copies:
        cp.wait()


def place(hops, blocks, full=None):
    args = [*map(vmem, blocks)] + ([] if full is None else [vmem(full)])
    return pl.pallas_call(
        functools.partial(place_kernel, hops, full is not None),
        out_shape=pltpu.VMEM((16, *blocks[0].shape[1:]), blocks[0].dtype),
        in_specs=[VM] * len(args),
        out_specs=VM,
        scratch_shapes=[pltpu.SemaphoreType.DMA((len(hops),))],
        input_output_aliases={} if full is None else {len(hops): 0},
        compiler_params=params(1),
        cost_estimate=cost(10**6),
    )(*args)


def sum_kernel(jobs, n_r, n_acc, k, *refs):
    rs, accs, outs = refs[:n_r], refs[n_r : n_r + n_acc], refs[n_r + n_acc :]
    z, _, x, c = position()
    ahead = (x - z) * (1 - 2 * c) + 4

    def tile(t, carry):
        rows = pl.ds(t * TILE, TILE)

        def add(out, half, pieces, start):
            cols = slice(half * 512, (half + 1) * 512)
            total = start[rows, cols]
            for r, row0, col0, at in pieces:
                total += jnp.dot(
                    k[root_index(*at), rows, :],
                    rs[r][row0 : row0 + 256, col0 : col0 + 512],
                    preferred_element_type=jnp.float32,
                )
            out[rows, cols] = total

        for out, (acc, hops, terms) in zip(outs, jobs):
            if hops is None:
                for half, pieces in enumerate(terms):
                    add(out, half, pieces, accs[acc])
                continue
            if acc is None:
                out[rows, :] = jnp.zeros((TILE, 1024), jnp.float32)
            for i in range(4):
                hop = (ahead + i) % 4

                @pl.when((hop >= hops[0]) & (hop <= hops[1]))
                def _():
                    for half, pieces in enumerate(terms):
                        here = [p for p in pieces if p[3][0] == i]
                        if here:
                            add(out, half, here, out)

        return carry

    lax.fori_loop(0, outs[0].shape[0] // TILE, tile, 0)


def sums(jobs, rs, k, accs):
    rows = k.shape[1]
    args = [*map(vmem, (k, *rs, *accs))]
    first = 1 + len(rs)
    return pl.pallas_call(
        functools.partial(sum_kernel, jobs, len(rs), len(accs)),
        out_shape=tuple(pltpu.VMEM((rows, 1024), jnp.float32) for _ in jobs),
        in_specs=[VM] * len(args),
        out_specs=tuple(VM for _ in jobs),
        input_output_aliases={first + acc: o for o, (acc, _, _) in enumerate(jobs) if acc is not None},
        compiler_params=params(8),
        cost_estimate=cost(10**6),
    )(*args)


def last_kernel(halves, n_r, k, *refs):
    rs, (acc, other, out, buf, sems) = refs[:n_r], refs[n_r:]
    copies = []
    for t in range(acc.shape[0] // TILE):
        rows = slice(t * TILE, (t + 1) * TILE)
        for half, pieces in enumerate(halves):
            cols = slice(half * 512, (half + 1) * 512)
            total = acc[rows, cols] + other[rows, cols]
            for r, row0, col0, at in pieces:
                total += jnp.dot(
                    k[root_index(*at), rows, :],
                    rs[r][row0 : row0 + 256, col0 : col0 + 512],
                    preferred_element_type=jnp.float32,
                )
            buf[rows, cols] = total
        cp = pltpu.make_async_copy(buf.at[pl.ds(t * TILE, TILE), :], out.at[pl.ds(t * TILE, TILE), :], sems.at[t])
        cp.start()
        copies.append(cp)
    for cp in copies:
        cp.wait()


def last(halves, rs, k, acc, other):
    rows = k.shape[1]
    args = [*map(vmem, (k, *rs, acc, other))]
    return pl.pallas_call(
        functools.partial(last_kernel, halves, len(rs)),
        out_shape=jax.ShapeDtypeStruct((rows, 1024), jnp.float32),
        in_specs=[VM] * len(args),
        out_specs=ANY,
        scratch_shapes=[pltpu.VMEM((rows, 1024), jnp.float32), pltpu.SemaphoreType.DMA((rows // TILE,))],
        compiler_params=params(8),
        cost_estimate=cost(10**6),
    )(*args)


def shards(library_bits, library_count, landmark_bits, landmark_count, inverse_root):
    core = lax.axis_index("lmk") % NC
    mine = lax.dynamic_slice_in_dim(inverse_root, core * 256, 256, 0)
    theirs = send(lax.dynamic_slice_in_dim(inverse_root, (1 - core) * 256, 256, 0), "core")
    row_scale = 0.9 * library_count.astype(jnp.float32)[:, None]
    col_scale = 0.1 * landmark_count.astype(jnp.float32)[None, :]
    row_bits, col_bits, token = load(library_bits, landmark_bits)
    theirs, swapped = lax.optimization_barrier((theirs, pick(landmark_bits)))
    own = [theirs, mine]
    first = [[[], []] for _ in range(2)]
    second = [[[], []] for _ in range(2)]
    for s in range(2):
        first[s][0].append(send(own[s], "y"))
        first[s][1].append(send(own[s], "z"))
    ks = [tversky(row_bits, row_scale, col_bits, col_scale, send(swapped, "core"))]

    def second_terms(hop, p):
        return [[(p, 256 * m, 0, (hop, m + 1)) for m in range(3)], [(p + 1, 256 * m, 0, (m + 1, hop)) for m in range(3)]]

    def first_terms(s, p):
        rs = [own[s], *first[s][0], *first[s][1], second[s][0][0], second[s][1][0]]
        where = [(0, 0), (0, 1), (0, 2), (0, 3), (1, 0), (2, 0), (3, 0)]
        more = second_terms(1, p + 7)
        return [[(p + n, 0, 512 * h, at) for n, at in enumerate(where)] + more[h] for h in range(2)], rs

    for step in range(10):
        s, hop = step % 2, step // 2
        rings = (first if hop < 3 else second)[s]
        ready = [rings[0][hop % 3], rings[1][hop % 3]]
        if step == 8:
            k = place([0, 1, 2], ks[:3])
            terms, rs = first_terms(0, 0)
            (acc,) = sums([(None, (0, 2), terms)], rs, k, [])
            ready.append(acc)
        if step == 9:
            terms, rs = first_terms(1, 0)
            jobs = [(None, (0, 2), terms), (0, (0, 2), second_terms(2, len(rs)))]
            other, acc = sums(jobs, [*rs, second[0][0][1], second[0][1][1]], k, [acc])
            ready.append(other)
        if step in (X1, X2):
            ready.append(ks[-1])
        token, *done = tie(token, *ready, flops=TIES[step] * 10**9)
        rings[0][hop % 3], rings[1][hop % 3] = done[:2]
        if step == 8:
            acc = done[2]
        if step == 9:
            other = done[2]
        if step in (X1, X2):
            ks[-1] = done[2]
        if hop < 2:
            rings[0].append(send(done[0], "y"))
            rings[1].append(send(done[1], "z"))
        elif hop == 2:
            left = jnp.concatenate([q[:, :512] for q in rings[0]])
            right = jnp.concatenate([q[:, 512:] for q in rings[1]])
            second[s][0].append(send(left, "z"))
            second[s][1].append(send(right, "y"))
        elif hop < 5:
            rings[0].append(send(done[0], "z"))
            rings[1].append(send(done[1], "y"))
        if step in (0, X1, X2):
            ks.append(send(ks[-1], "x"))

    k = place([3], ks[3:], k)
    terms, rs = first_terms(0, 0)
    more = second_terms(2, len(rs))
    terms = [terms[h] + more[h] for h in range(2)]
    (acc,) = sums([(0, (3, 3), terms)], [*rs, second[0][0][1], second[0][1][1]], k, [acc])
    (acc,) = sums([(0, None, second_terms(3, 0))], [second[0][0][2], second[0][1][2]], k, [acc])
    theirs = send(acc, "core")
    terms, rs = first_terms(1, 0)
    (other,) = sums([(0, (3, 3), terms)], rs, k, [other])
    (other,) = sums([(0, None, second_terms(2, 0))], [second[1][0][1], second[1][1][1]], k, [other])
    tail = tie(second[1][0][2], second[1][1][2], flops=TAIL)
    return last(second_terms(3, 0), tail, k, other, theirs)


def solution(mesh):
    placed = (P("lib", None), P("lib"), P("lmk", None), P("lmk"), P("lib", "lmk"))
    return jax.shard_map(
        shards, mesh=mesh, in_specs=placed, out_specs=P("lib", "lmk"), check_vma=False
    )
```

```python
import functools

import jax
import jax.numpy as jnp
from jax import lax
from jax.experimental import pallas as pl
from jax.experimental.pallas import tpu as pltpu
from jax.sharding import PartitionSpec as P

AXES = ("lib", "lmk")
NZ, NY, NX, NC = 4, 4, 4, 2
TILE = 256
TIES = [5, 5, 5, 5, 5, 6, 6, 6, 9, 9, 9]
TAIL = 5 * 10**10
X1 = 4
X2 = 7
TV = 10**6
LD = 10**6


def pairs_of(move):
    pairs = []
    for z in range(NZ):
        for y in range(NY):
            for x in range(NX):
                for c in range(NC):
                    tz, ty, tx, tc = move(z, y, x, c, 1 if c == 0 else -1)
                    to = ((tz % NZ * NY + ty % NY) * NX + tx % NX) * NC + tc
                    pairs.append((((z * NY + y) * NX + x) * NC + c, to))
    return pairs


PAIRS = {
    "z": pairs_of(lambda z, y, x, c, s: (z + s, y, x, c)),
    "y": pairs_of(lambda z, y, x, c, s: (z, y + s, x, c)),
    "x": pairs_of(lambda z, y, x, c, s: (z, y, x + s, c)),
    "core": pairs_of(lambda z, y, x, c, s: (z, y, x, 1 - c)),
}


def send(block, axis):
    return lax.ppermute(block, AXES, PAIRS[axis])


def vmem(x):
    return pltpu.with_memory_space_constraint(x, pltpu.VMEM)


def hbm(x):
    return pltpu.with_memory_space_constraint(x, pltpu.HBM)


def position():
    lib, lmk = lax.axis_index("lib"), lax.axis_index("lmk")
    return lib // NY, lib % NY, lmk // NC, lmk % NC


def root_index(i, j):
    z, y, _, c = position()
    back = 3 + 2 * c
    return (z + i * back) % NZ * NY + (y + j * back) % NY


def kernel_index(i):
    _, _, x, c = position()
    return (x + i * (3 + 2 * c)) % NX * 4


VM = pl.BlockSpec(memory_space=pltpu.VMEM)
ANY = pl.BlockSpec(memory_space=pl.ANY)


def params(mib):
    return pltpu.CompilerParams(vmem_limit_bytes=mib * 2**20)


def cost(flops, bytes_accessed=0):
    return pl.CostEstimate(flops=flops, bytes_accessed=bytes_accessed, transcendentals=0)


def load_kernel(row_bits, col_bits, rbuf, cbuf, token, sems):
    core = position()[3]
    copies = [pltpu.make_async_copy(row_bits, rbuf, sems.at[0])] + [
        pltpu.make_async_copy(
            col_bits.at[pl.ds(pl.multiple_of(h * 512 + core * 256, 256), 256), :],
            cbuf.at[pl.ds(h * 256, 256), :],
            sems.at[1 + h],
        )
        for h in range(2)
    ]
    for cp in copies:
        cp.start()
    token[...] = jnp.zeros(token.shape, token.dtype)
    for cp in copies:
        cp.wait()


def load(row_bits, col_bits):
    rows, depth = row_bits.shape
    return pl.pallas_call(
        load_kernel,
        out_shape=(
            pltpu.VMEM((rows, depth), jnp.bfloat16),
            pltpu.VMEM((512, depth), jnp.bfloat16),
            pltpu.VMEM((16, 128), jnp.bfloat16),
        ),
        in_specs=[ANY, ANY],
        out_specs=(VM,) * 3,
        scratch_shapes=[pltpu.SemaphoreType.DMA((3,))],
        compiler_params=params(1),
        cost_estimate=cost(LD),
    )(hbm(row_bits), hbm(col_bits))


def pick_kernel(col_bits, out, sems):
    core = position()[3]
    copies = [
        pltpu.make_async_copy(
            col_bits.at[pl.ds(pl.multiple_of(h * 512 + (1 - core) * 256, 256), 256), :],
            out.at[pl.ds(h * 256, 256), :],
            sems.at[h],
        )
        for h in range(2)
    ]
    for cp in copies:
        cp.start()
    for cp in copies:
        cp.wait()


def pick(col_bits):
    return pl.pallas_call(
        pick_kernel,
        out_shape=pltpu.VMEM((512, col_bits.shape[1]), col_bits.dtype),
        in_specs=[ANY],
        out_specs=VM,
        scratch_shapes=[pltpu.SemaphoreType.DMA((2,))],
        compiler_params=params(1),
        cost_estimate=cost(10**6),
    )(hbm(col_bits))


def tversky_kernel(row_bits, row_scale, col_bits, col_scale, got_bits, out, ones):
    core = position()[3]
    nt = (((1,), (1,)), ((), ()))
    ones[...] = jnp.ones(ones.shape, ones.dtype)
    for part, bits_ref in enumerate((col_bits, got_bits)):
        for h in range(2):
            bits = bits_ref[h * 256 : (h + 1) * 256, :]
            if part == 0:
                scale, to = col_scale[:, pl.ds(pl.multiple_of(h * 512 + core * 256, 256), 256)], 2 * core + h
            else:
                count = lax.dot_general(ones[...], bits, nt, preferred_element_type=jnp.float32)[:1, :]
                scale, to = 0.1 * count, 2 * (1 - core) + h
            for t in range(row_bits.shape[0] // TILE):
                rows = slice(t * TILE, (t + 1) * TILE)
                common = lax.dot_general(row_bits[rows, :], bits, nt, preferred_element_type=jnp.float32)
                out[to, rows, :] = (common / (row_scale[rows, :] + scale)).astype(jnp.bfloat16)


def tversky(row_bits, row_scale, col_bits, col_scale, got_bits):
    rows, depth = row_bits.shape
    return pl.pallas_call(
        tversky_kernel,
        out_shape=pltpu.VMEM((4, rows, 256), jnp.bfloat16),
        in_specs=[VM] * 5,
        out_specs=VM,
        scratch_shapes=[pltpu.VMEM((TILE, depth), jnp.bfloat16)],
        compiler_params=params(8),
        cost_estimate=cost(TV),
    )(*map(vmem, (row_bits, row_scale, col_bits, col_scale, got_bits)))


def tie_kernel(*refs):
    pass


def tie(*arrays, flops):
    return pl.pallas_call(
        tie_kernel,
        out_shape=tuple(pltpu.VMEM(a.shape, a.dtype) for a in arrays),
        in_specs=[VM] * len(arrays),
        out_specs=(VM,) * len(arrays),
        input_output_aliases={i: i for i in range(len(arrays))},
        compiler_params=params(1),
        cost_estimate=cost(flops),
    )(*map(vmem, arrays))


def place_kernel(hops, has_full, *refs):
    n = len(hops)
    blocks, full, sems = refs[:n], refs[n + has_full], refs[n + has_full + 1]
    copies = [
        pltpu.make_async_copy(b, full.at[pl.ds(kernel_index(i), 4)], sems.at[at])
        for at, (i, b) in enumerate(zip(hops, blocks))
    ]
    for cp in copies:
        cp.start()
    for cp in copies:
        cp.wait()


def place(hops, blocks, full=None):
    args = [*map(vmem, blocks)] + ([] if full is None else [vmem(full)])
    return pl.pallas_call(
        functools.partial(place_kernel, hops, full is not None),
        out_shape=pltpu.VMEM((16, *blocks[0].shape[1:]), blocks[0].dtype),
        in_specs=[VM] * len(args),
        out_specs=VM,
        scratch_shapes=[pltpu.SemaphoreType.DMA((len(hops),))],
        input_output_aliases={} if full is None else {len(hops): 0},
        compiler_params=params(1),
        cost_estimate=cost(10**6),
    )(*args)


def sum_kernel(jobs, n_r, n_acc, k, *refs):
    rs, accs, outs = refs[:n_r], refs[n_r : n_r + n_acc], refs[n_r + n_acc :]
    z, _, x, c = position()
    ahead = (x - z) * (1 - 2 * c) + 4

    def tile(t, carry):
        rows = pl.ds(t * TILE, TILE)

        def add(out, half, pieces, start):
            cols = slice(half * 512, (half + 1) * 512)
            total = start[rows, cols]
            for r, row0, col0, at in pieces:
                total += jnp.dot(
                    k[root_index(*at), rows, :],
                    rs[r][row0 : row0 + 256, col0 : col0 + 512],
                    preferred_element_type=jnp.float32,
                )
            out[rows, cols] = total

        for out, (acc, hops, terms) in zip(outs, jobs):
            if hops is None:
                for half, pieces in enumerate(terms):
                    add(out, half, pieces, accs[acc])
                continue
            if acc is None:
                out[rows, :] = jnp.zeros((TILE, 1024), jnp.float32)
            for i in range(4):
                hop = (ahead + i) % 4

                @pl.when((hop >= hops[0]) & (hop <= hops[1]))
                def _():
                    for half, pieces in enumerate(terms):
                        here = [p for p in pieces if p[3][0] == i]
                        if here:
                            add(out, half, here, out)

        return carry

    lax.fori_loop(0, outs[0].shape[0] // TILE, tile, 0)


def sums(jobs, rs, k, accs):
    rows = k.shape[1]
    args = [*map(vmem, (k, *rs, *accs))]
    first = 1 + len(rs)
    return pl.pallas_call(
        functools.partial(sum_kernel, jobs, len(rs), len(accs)),
        out_shape=tuple(pltpu.VMEM((rows, 1024), jnp.float32) for _ in jobs),
        in_specs=[VM] * len(args),
        out_specs=tuple(VM for _ in jobs),
        input_output_aliases={first + acc: o for o, (acc, _, _) in enumerate(jobs) if acc is not None},
        compiler_params=params(8),
        cost_estimate=cost(10**6),
    )(*args)


def last_kernel(halves, n_r, k, *refs):
    rs, (acc, other, out, buf, sems) = refs[:n_r], refs[n_r:]
    copies = []
    for t in range(acc.shape[0] // TILE):
        rows = slice(t * TILE, (t + 1) * TILE)
        for half, pieces in enumerate(halves):
            cols = slice(half * 512, (half + 1) * 512)
            total = acc[rows, cols] + other[rows, cols]
            for r, row0, col0, at in pieces:
                total += jnp.dot(
                    k[root_index(*at), rows, :],
                    rs[r][row0 : row0 + 256, col0 : col0 + 512],
                    preferred_element_type=jnp.float32,
                )
            buf[rows, cols] = total
            at = (pl.ds(t * TILE, TILE), pl.ds(half * 512, 512))
            cp = pltpu.make_async_copy(buf.at[at], out.at[at], sems.at[2 * t + half])
            cp.start()
            copies.append(cp)
    for cp in copies:
        cp.wait()


def last(halves, rs, k, acc, other):
    rows = k.shape[1]
    args = [*map(vmem, (k, *rs, acc, other))]
    return pl.pallas_call(
        functools.partial(last_kernel, halves, len(rs)),
        out_shape=jax.ShapeDtypeStruct((rows, 1024), jnp.float32),
        in_specs=[VM] * len(args),
        out_specs=ANY,
        scratch_shapes=[pltpu.VMEM((rows, 1024), jnp.float32), pltpu.SemaphoreType.DMA((2 * (rows // TILE),))],
        compiler_params=params(8),
        cost_estimate=cost(10**6),
    )(*args)


def shards(library_bits, library_count, landmark_bits, landmark_count, inverse_root):
    core = lax.axis_index("lmk") % NC
    mine = lax.dynamic_slice_in_dim(inverse_root, core * 256, 256, 0)
    theirs = send(lax.dynamic_slice_in_dim(inverse_root, (1 - core) * 256, 256, 0), "core")
    row_scale = 0.9 * library_count.astype(jnp.float32)[:, None]
    col_scale = 0.1 * landmark_count.astype(jnp.float32)[None, :]
    row_bits, col_bits, token = load(library_bits, landmark_bits)
    theirs, swapped = lax.optimization_barrier((theirs, pick(landmark_bits)))
    own = [theirs, mine]
    first = [[[], []] for _ in range(2)]
    second = [[[], []] for _ in range(2)]
    for s in range(2):
        first[s][0].append(send(own[s], "y"))
        first[s][1].append(send(own[s], "z"))
    ks = [tversky(row_bits, row_scale, col_bits, col_scale, send(swapped, "core"))]

    def second_terms(hop, p):
        return [[(p, 256 * m, 0, (hop, m + 1)) for m in range(3)], [(p + 1, 256 * m, 0, (m + 1, hop)) for m in range(3)]]

    def first_terms(s, p):
        rs = [own[s], *first[s][0], *first[s][1], second[s][0][0], second[s][1][0]]
        where = [(0, 0), (0, 1), (0, 2), (0, 3), (1, 0), (2, 0), (3, 0)]
        more = second_terms(1, p + 7)
        return [[(p + n, 0, 512 * h, at) for n, at in enumerate(where)] + more[h] for h in range(2)], rs

    for step in range(10):
        s, hop = step % 2, step // 2
        rings = (first if hop < 3 else second)[s]
        ready = [rings[0][hop % 3], rings[1][hop % 3]]
        if step == 8:
            k = place([0, 1, 2], ks[:3])
            terms, rs = first_terms(0, 0)
            (acc,) = sums([(None, (0, 2), terms)], rs, k, [])
            ready.append(acc)
        if step == 9:
            terms, rs = first_terms(1, 0)
            jobs = [(None, (0, 2), terms), (0, (0, 2), second_terms(2, len(rs)))]
            other, acc = sums(jobs, [*rs, second[0][0][1], second[0][1][1]], k, [acc])
            ready.append(other)
        if step in (X1, X2):
            ready.append(ks[-1])
        token, *done = tie(token, *ready, flops=TIES[step] * 10**9)
        rings[0][hop % 3], rings[1][hop % 3] = done[:2]
        if step == 8:
            acc = done[2]
        if step == 9:
            other = done[2]
        if step in (X1, X2):
            ks[-1] = done[2]
        if hop < 2:
            rings[0].append(send(done[0], "y"))
            rings[1].append(send(done[1], "z"))
        elif hop == 2:
            left = jnp.concatenate([q[:, :512] for q in rings[0]])
            right = jnp.concatenate([q[:, 512:] for q in rings[1]])
            second[s][0].append(send(left, "z"))
            second[s][1].append(send(right, "y"))
        elif hop < 5:
            rings[0].append(send(done[0], "z"))
            rings[1].append(send(done[1], "y"))
        if step in (0, X1, X2):
            ks.append(send(ks[-1], "x"))

    k = place([3], ks[3:], k)
    terms, rs = first_terms(0, 0)
    more = second_terms(2, len(rs))
    terms = [terms[h] + more[h] for h in range(2)]
    (acc,) = sums([(0, (3, 3), terms)], [*rs, second[0][0][1], second[0][1][1]], k, [acc])
    (acc,) = sums([(0, None, second_terms(3, 0))], [second[0][0][2], second[0][1][2]], k, [acc])
    theirs = send(acc, "core")
    terms, rs = first_terms(1, 0)
    (other,) = sums([(0, (3, 3), terms)], rs, k, [other])
    (other,) = sums([(0, None, second_terms(2, 0))], [second[1][0][1], second[1][1][1]], k, [other])
    tail = tie(second[1][0][2], second[1][1][2], flops=TAIL)
    return last(second_terms(3, 0), tail, k, other, theirs)


def solution(mesh):
    placed = (P("lib", None), P("lib"), P("lmk", None), P("lmk"), P("lib", "lmk"))
    return jax.shard_map(
        shards, mesh=mesh, in_specs=placed, out_specs=P("lib", "lmk"), check_vma=False
    )
```

```python
import functools

import jax
import jax.numpy as jnp
from jax import lax
from jax.experimental import pallas as pl
from jax.experimental.pallas import tpu as pltpu
from jax.sharding import PartitionSpec as P

AXES = ("lib", "lmk")
NZ, NY, NX, NC = 4, 4, 4, 2
TILE = 256
TIES = [5, 5, 5, 5, 5, 6, 6, 6, 9, 9, 9]
TAIL = 5 * 10**10
X1 = 4
X2 = 7
TV = 10**6
LD = 10**6


def pairs_of(move):
    pairs = []
    for z in range(NZ):
        for y in range(NY):
            for x in range(NX):
                for c in range(NC):
                    tz, ty, tx, tc = move(z, y, x, c, 1 if c == 0 else -1)
                    to = ((tz % NZ * NY + ty % NY) * NX + tx % NX) * NC + tc
                    pairs.append((((z * NY + y) * NX + x) * NC + c, to))
    return pairs


PAIRS = {
    "z": pairs_of(lambda z, y, x, c, s: (z + s, y, x, c)),
    "y": pairs_of(lambda z, y, x, c, s: (z, y + s, x, c)),
    "x": pairs_of(lambda z, y, x, c, s: (z, y, x + s, c)),
    "core": pairs_of(lambda z, y, x, c, s: (z, y, x, 1 - c)),
}


def send(block, axis):
    return lax.ppermute(block, AXES, PAIRS[axis])


def vmem(x):
    return pltpu.with_memory_space_constraint(x, pltpu.VMEM)


def hbm(x):
    return pltpu.with_memory_space_constraint(x, pltpu.HBM)


def position():
    lib, lmk = lax.axis_index("lib"), lax.axis_index("lmk")
    return lib // NY, lib % NY, lmk // NC, lmk % NC


def root_index(i, j):
    z, y, _, c = position()
    back = 3 + 2 * c
    return (z + i * back) % NZ * NY + (y + j * back) % NY


def kernel_index(i):
    _, _, x, c = position()
    return (x + i * (3 + 2 * c)) % NX * 4


VM = pl.BlockSpec(memory_space=pltpu.VMEM)
ANY = pl.BlockSpec(memory_space=pl.ANY)


def params(mib):
    return pltpu.CompilerParams(vmem_limit_bytes=mib * 2**20)


def cost(flops, bytes_accessed=0):
    return pl.CostEstimate(flops=flops, bytes_accessed=bytes_accessed, transcendentals=0)


def load_kernel(row_bits, col_bits, rbuf, cbuf, token, sems):
    core = position()[3]
    copies = [pltpu.make_async_copy(row_bits, rbuf, sems.at[0])] + [
        pltpu.make_async_copy(
            col_bits.at[pl.ds(pl.multiple_of(h * 512 + core * 256, 256), 256), :],
            cbuf.at[pl.ds(h * 256, 256), :],
            sems.at[1 + h],
        )
        for h in range(2)
    ]
    for cp in copies:
        cp.start()
    token[...] = jnp.zeros(token.shape, token.dtype)
    for cp in copies:
        cp.wait()


def load(row_bits, col_bits):
    rows, depth = row_bits.shape
    return pl.pallas_call(
        load_kernel,
        out_shape=(
            pltpu.VMEM((rows, depth), jnp.bfloat16),
            pltpu.VMEM((512, depth), jnp.bfloat16),
            pltpu.VMEM((16, 128), jnp.bfloat16),
        ),
        in_specs=[ANY, ANY],
        out_specs=(VM,) * 3,
        scratch_shapes=[pltpu.SemaphoreType.DMA((3,))],
        compiler_params=params(1),
        cost_estimate=cost(LD),
    )(hbm(row_bits), hbm(col_bits))


def pick_kernel(col_bits, out, sems):
    core = position()[3]
    copies = [
        pltpu.make_async_copy(
            col_bits.at[pl.ds(pl.multiple_of(h * 512 + (1 - core) * 256, 256), 256), :],
            out.at[pl.ds(h * 256, 256), :],
            sems.at[h],
        )
        for h in range(2)
    ]
    for cp in copies:
        cp.start()
    for cp in copies:
        cp.wait()


def pick(col_bits):
    return pl.pallas_call(
        pick_kernel,
        out_shape=pltpu.VMEM((512, col_bits.shape[1]), col_bits.dtype),
        in_specs=[ANY],
        out_specs=VM,
        scratch_shapes=[pltpu.SemaphoreType.DMA((2,))],
        compiler_params=params(1),
        cost_estimate=cost(10**6),
    )(hbm(col_bits))


def other_rows_kernel(block, out, sems):
    at = pl.multiple_of((1 - position()[3]) * 256, 256)
    copy = pltpu.make_async_copy(block.at[pl.ds(at, 256), :], out, sems.at[0])
    copy.start()
    copy.wait()


def other_rows(block):
    return pl.pallas_call(
        other_rows_kernel,
        out_shape=pltpu.VMEM((256, block.shape[1]), block.dtype),
        in_specs=[ANY],
        out_specs=VM,
        scratch_shapes=[pltpu.SemaphoreType.DMA((1,))],
        compiler_params=params(1),
        cost_estimate=cost(10**6),
    )(hbm(block))


def tversky_kernel(row_bits, row_scale, col_bits, col_scale, got_bits, out, ones):
    core = position()[3]
    nt = (((1,), (1,)), ((), ()))
    ones[...] = jnp.ones(ones.shape, ones.dtype)
    for part, bits_ref in enumerate((col_bits, got_bits)):
        for h in range(2):
            bits = bits_ref[h * 256 : (h + 1) * 256, :]
            if part == 0:
                scale, to = col_scale[:, pl.ds(pl.multiple_of(h * 512 + core * 256, 256), 256)], 2 * core + h
            else:
                count = lax.dot_general(ones[...], bits, nt, preferred_element_type=jnp.float32)[:1, :]
                scale, to = 0.1 * count, 2 * (1 - core) + h
            for t in range(row_bits.shape[0] // TILE):
                rows = slice(t * TILE, (t + 1) * TILE)
                common = lax.dot_general(row_bits[rows, :], bits, nt, preferred_element_type=jnp.float32)
                out[to, rows, :] = (common / (row_scale[rows, :] + scale)).astype(jnp.bfloat16)


def tversky(row_bits, row_scale, col_bits, col_scale, got_bits):
    rows, depth = row_bits.shape
    return pl.pallas_call(
        tversky_kernel,
        out_shape=pltpu.VMEM((4, rows, 256), jnp.bfloat16),
        in_specs=[VM] * 5,
        out_specs=VM,
        scratch_shapes=[pltpu.VMEM((TILE, depth), jnp.bfloat16)],
        compiler_params=params(8),
        cost_estimate=cost(TV),
    )(*map(vmem, (row_bits, row_scale, col_bits, col_scale, got_bits)))


def tie_kernel(*refs):
    pass


def tie(*arrays, flops):
    return pl.pallas_call(
        tie_kernel,
        out_shape=tuple(pltpu.VMEM(a.shape, a.dtype) for a in arrays),
        in_specs=[VM] * len(arrays),
        out_specs=(VM,) * len(arrays),
        input_output_aliases={i: i for i in range(len(arrays))},
        compiler_params=params(1),
        cost_estimate=cost(flops),
    )(*map(vmem, arrays))


def place_kernel(hops, has_full, *refs):
    n = len(hops)
    blocks, full, sems = refs[:n], refs[n + has_full], refs[n + has_full + 1]
    copies = [
        pltpu.make_async_copy(b, full.at[pl.ds(kernel_index(i), 4)], sems.at[at])
        for at, (i, b) in enumerate(zip(hops, blocks))
    ]
    for cp in copies:
        cp.start()
    for cp in copies:
        cp.wait()


def place(hops, blocks, full=None):
    args = [*map(vmem, blocks)] + ([] if full is None else [vmem(full)])
    return pl.pallas_call(
        functools.partial(place_kernel, hops, full is not None),
        out_shape=pltpu.VMEM((16, *blocks[0].shape[1:]), blocks[0].dtype),
        in_specs=[VM] * len(args),
        out_specs=VM,
        scratch_shapes=[pltpu.SemaphoreType.DMA((len(hops),))],
        input_output_aliases={} if full is None else {len(hops): 0},
        compiler_params=params(1),
        cost_estimate=cost(10**6),
    )(*args)


def sum_kernel(jobs, n_r, n_acc, k, *refs):
    rs, accs, outs = refs[:n_r], refs[n_r : n_r + n_acc], refs[n_r + n_acc :]
    z, _, x, c = position()
    ahead = (x - z) * (1 - 2 * c) + 4

    def tile(t, carry):
        rows = pl.ds(t * TILE, TILE)

        def add(out, half, pieces, start):
            cols = slice(half * 512, (half + 1) * 512)
            total = start[rows, cols]
            for r, row0, col0, at in pieces:
                total += jnp.dot(
                    k[root_index(*at), rows, :],
                    rs[r][row0 : row0 + 256, col0 : col0 + 512],
                    preferred_element_type=jnp.float32,
                )
            out[rows, cols] = total

        for out, (acc, hops, terms) in zip(outs, jobs):
            if hops is None:
                for half, pieces in enumerate(terms):
                    add(out, half, pieces, accs[acc])
                continue
            if acc is None:
                out[rows, :] = jnp.zeros((TILE, 1024), jnp.float32)
            for i in range(4):
                hop = (ahead + i) % 4

                @pl.when((hop >= hops[0]) & (hop <= hops[1]))
                def _():
                    for half, pieces in enumerate(terms):
                        here = [p for p in pieces if p[3][0] == i]
                        if here:
                            add(out, half, here, out)

        return carry

    lax.fori_loop(0, outs[0].shape[0] // TILE, tile, 0)


def sums(jobs, rs, k, accs):
    rows = k.shape[1]
    args = [*map(vmem, (k, *rs, *accs))]
    first = 1 + len(rs)
    return pl.pallas_call(
        functools.partial(sum_kernel, jobs, len(rs), len(accs)),
        out_shape=tuple(pltpu.VMEM((rows, 1024), jnp.float32) for _ in jobs),
        in_specs=[VM] * len(args),
        out_specs=tuple(VM for _ in jobs),
        input_output_aliases={first + acc: o for o, (acc, _, _) in enumerate(jobs) if acc is not None},
        compiler_params=params(8),
        cost_estimate=cost(10**6),
    )(*args)


def last_kernel(halves, n_r, k, *refs):
    rs, (acc, other, out, buf, sems) = refs[:n_r], refs[n_r:]
    copies = []
    for t in range(acc.shape[0] // TILE):
        rows = slice(t * TILE, (t + 1) * TILE)
        for half, pieces in enumerate(halves):
            cols = slice(half * 512, (half + 1) * 512)
            total = acc[rows, cols] + other[rows, cols]
            for r, row0, col0, at in pieces:
                total += jnp.dot(
                    k[root_index(*at), rows, :],
                    rs[r][row0 : row0 + 256, col0 : col0 + 512],
                    preferred_element_type=jnp.float32,
                )
            buf[rows, cols] = total
            at = (pl.ds(t * TILE, TILE), pl.ds(half * 512, 512))
            cp = pltpu.make_async_copy(buf.at[at], out.at[at], sems.at[2 * t + half])
            cp.start()
            copies.append(cp)
    for cp in copies:
        cp.wait()


def last(halves, rs, k, acc, other):
    rows = k.shape[1]
    args = [*map(vmem, (k, *rs, acc, other))]
    return pl.pallas_call(
        functools.partial(last_kernel, halves, len(rs)),
        out_shape=jax.ShapeDtypeStruct((rows, 1024), jnp.float32),
        in_specs=[VM] * len(args),
        out_specs=ANY,
        scratch_shapes=[pltpu.VMEM((rows, 1024), jnp.float32), pltpu.SemaphoreType.DMA((2 * (rows // TILE),))],
        compiler_params=params(8),
        cost_estimate=cost(10**6),
    )(*args)


def shards(library_bits, library_count, landmark_bits, landmark_count, inverse_root):
    core = lax.axis_index("lmk") % NC
    mine = lax.dynamic_slice_in_dim(inverse_root, core * 256, 256, 0)
    theirs = send(other_rows(inverse_root), "core")
    row_scale = 0.9 * library_count.astype(jnp.float32)[:, None]
    col_scale = 0.1 * landmark_count.astype(jnp.float32)[None, :]
    row_bits, col_bits, token = load(library_bits, landmark_bits)
    theirs, swapped = lax.optimization_barrier((theirs, pick(landmark_bits)))
    own = [theirs, mine]
    first = [[[], []] for _ in range(2)]
    second = [[[], []] for _ in range(2)]
    for s in range(2):
        first[s][0].append(send(own[s], "y"))
        first[s][1].append(send(own[s], "z"))
    ks = [tversky(row_bits, row_scale, col_bits, col_scale, send(swapped, "core"))]

    def second_terms(hop, p):
        return [[(p, 256 * m, 0, (hop, m + 1)) for m in range(3)], [(p + 1, 256 * m, 0, (m + 1, hop)) for m in range(3)]]

    def first_terms(s, p):
        rs = [own[s], *first[s][0], *first[s][1], second[s][0][0], second[s][1][0]]
        where = [(0, 0), (0, 1), (0, 2), (0, 3), (1, 0), (2, 0), (3, 0)]
        more = second_terms(1, p + 7)
        return [[(p + n, 0, 512 * h, at) for n, at in enumerate(where)] + more[h] for h in range(2)], rs

    for step in range(10):
        s, hop = step % 2, step // 2
        rings = (first if hop < 3 else second)[s]
        ready = [rings[0][hop % 3], rings[1][hop % 3]]
        if step == 8:
            k = place([0, 1, 2], ks[:3])
            terms, rs = first_terms(0, 0)
            (acc,) = sums([(None, (0, 2), terms)], rs, k, [])
            ready.append(acc)
        if step == 9:
            terms, rs = first_terms(1, 0)
            jobs = [(None, (0, 2), terms), (0, (0, 2), second_terms(2, len(rs)))]
            other, acc = sums(jobs, [*rs, second[0][0][1], second[0][1][1]], k, [acc])
            ready.append(other)
        if step in (X1, X2):
            ready.append(ks[-1])
        token, *done = tie(token, *ready, flops=TIES[step] * 10**9)
        rings[0][hop % 3], rings[1][hop % 3] = done[:2]
        if step == 8:
            acc = done[2]
        if step == 9:
            other = done[2]
        if step in (X1, X2):
            ks[-1] = done[2]
        if hop < 2:
            rings[0].append(send(done[0], "y"))
            rings[1].append(send(done[1], "z"))
        elif hop == 2:
            left = jnp.concatenate([q[:, :512] for q in rings[0]])
            right = jnp.concatenate([q[:, 512:] for q in rings[1]])
            second[s][0].append(send(left, "z"))
            second[s][1].append(send(right, "y"))
        elif hop < 5:
            rings[0].append(send(done[0], "z"))
            rings[1].append(send(done[1], "y"))
        if step in (0, X1, X2):
            ks.append(send(ks[-1], "x"))

    k = place([3], ks[3:], k)
    terms, rs = first_terms(0, 0)
    more = second_terms(2, len(rs))
    terms = [terms[h] + more[h] for h in range(2)]
    (acc,) = sums([(0, (3, 3), terms)], [*rs, second[0][0][1], second[0][1][1]], k, [acc])
    (acc,) = sums([(0, None, second_terms(3, 0))], [second[0][0][2], second[0][1][2]], k, [acc])
    theirs = send(acc, "core")
    terms, rs = first_terms(1, 0)
    (other,) = sums([(0, (3, 3), terms)], rs, k, [other])
    (other,) = sums([(0, None, second_terms(2, 0))], [second[1][0][1], second[1][1][1]], k, [other])
    tail = tie(second[1][0][2], second[1][1][2], flops=TAIL)
    return last(second_terms(3, 0), tail, k, other, theirs)


def solution(mesh):
    placed = (P("lib", None), P("lib"), P("lmk", None), P("lmk"), P("lib", "lmk"))
    return jax.shard_map(
        shards, mesh=mesh, in_specs=placed, out_specs=P("lib", "lmk"), check_vma=False
    )
```

```python
import functools

import jax
import jax.numpy as jnp
from jax import lax
from jax.experimental import pallas as pl
from jax.experimental.pallas import tpu as pltpu
from jax.sharding import PartitionSpec as P

AXES = ("lib", "lmk")
NZ, NY, NX, NC = 4, 4, 4, 2
TILE = 256
TIES = [5, 5, 5, 5, 5, 6, 6, 6, 9, 9, 9]
TAIL = 5 * 10**10
X1 = 4
X2 = 7
TV = 10**6
LD = 10**6


def pairs_of(move):
    pairs = []
    for z in range(NZ):
        for y in range(NY):
            for x in range(NX):
                for c in range(NC):
                    tz, ty, tx, tc = move(z, y, x, c, 1 if c == 0 else -1)
                    to = ((tz % NZ * NY + ty % NY) * NX + tx % NX) * NC + tc
                    pairs.append((((z * NY + y) * NX + x) * NC + c, to))
    return pairs


PAIRS = {
    "z": pairs_of(lambda z, y, x, c, s: (z + s, y, x, c)),
    "y": pairs_of(lambda z, y, x, c, s: (z, y + s, x, c)),
    "x": pairs_of(lambda z, y, x, c, s: (z, y, x + s, c)),
    "core": pairs_of(lambda z, y, x, c, s: (z, y, x, 1 - c)),
}


def send(block, axis):
    return lax.ppermute(block, AXES, PAIRS[axis])


def vmem(x):
    return pltpu.with_memory_space_constraint(x, pltpu.VMEM)


def hbm(x):
    return pltpu.with_memory_space_constraint(x, pltpu.HBM)


def position():
    lib, lmk = lax.axis_index("lib"), lax.axis_index("lmk")
    return lib // NY, lib % NY, lmk // NC, lmk % NC


def root_index(i, j):
    z, y, _, c = position()
    back = 3 + 2 * c
    return (z + i * back) % NZ * NY + (y + j * back) % NY


def kernel_index(i):
    _, _, x, c = position()
    return (x + i * (3 + 2 * c)) % NX * 4


VM = pl.BlockSpec(memory_space=pltpu.VMEM)
ANY = pl.BlockSpec(memory_space=pl.ANY)


def params(mib):
    return pltpu.CompilerParams(vmem_limit_bytes=mib * 2**20)


def cost(flops, bytes_accessed=0):
    return pl.CostEstimate(flops=flops, bytes_accessed=bytes_accessed, transcendentals=0)


def load_kernel(row_bits, col_bits, rbuf, cbuf, token, sems):
    core = position()[3]
    copies = [pltpu.make_async_copy(row_bits, rbuf, sems.at[0])] + [
        pltpu.make_async_copy(
            col_bits.at[pl.ds(pl.multiple_of(h * 512 + core * 256, 256), 256), :],
            cbuf.at[pl.ds(h * 256, 256), :],
            sems.at[1 + h],
        )
        for h in range(2)
    ]
    for cp in copies:
        cp.start()
    token[...] = jnp.zeros(token.shape, token.dtype)
    for cp in copies:
        cp.wait()


def load(row_bits, col_bits):
    rows, depth = row_bits.shape
    return pl.pallas_call(
        load_kernel,
        out_shape=(
            pltpu.VMEM((rows, depth), jnp.bfloat16),
            pltpu.VMEM((512, depth), jnp.bfloat16),
            pltpu.VMEM((16, 128), jnp.bfloat16),
        ),
        in_specs=[ANY, ANY],
        out_specs=(VM,) * 3,
        scratch_shapes=[pltpu.SemaphoreType.DMA((3,))],
        compiler_params=params(1),
        cost_estimate=cost(LD),
    )(hbm(row_bits), hbm(col_bits))


def pick_kernel(col_bits, out, sems):
    core = position()[3]
    copies = [
        pltpu.make_async_copy(
            col_bits.at[pl.ds(pl.multiple_of(h * 512 + (1 - core) * 256, 256), 256), :],
            out.at[pl.ds(h * 256, 256), :],
            sems.at[h],
        )
        for h in range(2)
    ]
    for cp in copies:
        cp.start()
    for cp in copies:
        cp.wait()


def pick(col_bits):
    return pl.pallas_call(
        pick_kernel,
        out_shape=pltpu.VMEM((512, col_bits.shape[1]), col_bits.dtype),
        in_specs=[ANY],
        out_specs=VM,
        scratch_shapes=[pltpu.SemaphoreType.DMA((2,))],
        compiler_params=params(1),
        cost_estimate=cost(10**6),
    )(hbm(col_bits))


def tversky_kernel(row_bits, row_scale, col_bits, col_scale, got_bits, out, ones):
    core = position()[3]
    nt = (((1,), (1,)), ((), ()))
    ones[...] = jnp.ones(ones.shape, ones.dtype)
    for part, bits_ref in enumerate((col_bits, got_bits)):
        for h in range(2):
            bits = bits_ref[h * 256 : (h + 1) * 256, :]
            if part == 0:
                scale, to = col_scale[:, pl.ds(pl.multiple_of(h * 512 + core * 256, 256), 256)], 2 * core + h
            else:
                count = lax.dot_general(ones[...], bits, nt, preferred_element_type=jnp.float32)[:1, :]
                scale, to = 0.1 * count, 2 * (1 - core) + h
            for t in range(row_bits.shape[0] // TILE):
                rows = slice(t * TILE, (t + 1) * TILE)
                common = lax.dot_general(row_bits[rows, :], bits, nt, preferred_element_type=jnp.float32)
                out[to, rows, :] = (common / (row_scale[rows, :] + scale)).astype(jnp.bfloat16)


def tversky(row_bits, row_scale, col_bits, col_scale, got_bits):
    rows, depth = row_bits.shape
    return pl.pallas_call(
        tversky_kernel,
        out_shape=pltpu.VMEM((4, rows, 256), jnp.bfloat16),
        in_specs=[VM] * 5,
        out_specs=VM,
        scratch_shapes=[pltpu.VMEM((TILE, depth), jnp.bfloat16)],
        compiler_params=params(8),
        cost_estimate=cost(TV),
    )(*map(vmem, (row_bits, row_scale, col_bits, col_scale, got_bits)))


def tie_kernel(*refs):
    pass


def tie(*arrays, flops):
    return pl.pallas_call(
        tie_kernel,
        out_shape=tuple(pltpu.VMEM(a.shape, a.dtype) for a in arrays),
        in_specs=[VM] * len(arrays),
        out_specs=(VM,) * len(arrays),
        input_output_aliases={i: i for i in range(len(arrays))},
        compiler_params=params(1),
        cost_estimate=cost(flops),
    )(*map(vmem, arrays))


def place_kernel(hops, has_full, *refs):
    n = len(hops)
    blocks, full, sems = refs[:n], refs[n + has_full], refs[n + has_full + 1]
    copies = [
        pltpu.make_async_copy(b, full.at[pl.ds(kernel_index(i), 4)], sems.at[at])
        for at, (i, b) in enumerate(zip(hops, blocks))
    ]
    for cp in copies:
        cp.start()
    for cp in copies:
        cp.wait()


def place(hops, blocks, full=None):
    args = [*map(vmem, blocks)] + ([] if full is None else [vmem(full)])
    return pl.pallas_call(
        functools.partial(place_kernel, hops, full is not None),
        out_shape=pltpu.VMEM((16, *blocks[0].shape[1:]), blocks[0].dtype),
        in_specs=[VM] * len(args),
        out_specs=VM,
        scratch_shapes=[pltpu.SemaphoreType.DMA((len(hops),))],
        input_output_aliases={} if full is None else {len(hops): 0},
        compiler_params=params(1),
        cost_estimate=cost(10**6),
    )(*args)


def sum_kernel(jobs, n_r, n_acc, k, *refs):
    rs, accs, outs = refs[:n_r], refs[n_r : n_r + n_acc], refs[n_r + n_acc :]
    z, _, x, c = position()
    ahead = (x - z) * (1 - 2 * c) + 4

    def tile(t, carry):
        rows = pl.ds(t * TILE, TILE)

        def add(out, half, pieces, start):
            cols = slice(half * 512, (half + 1) * 512)
            total = start[rows, cols]
            for r, row0, col0, at in pieces:
                total += jnp.dot(
                    k[root_index(*at), rows, :],
                    rs[r][row0 : row0 + 256, col0 : col0 + 512],
                    preferred_element_type=jnp.float32,
                )
            out[rows, cols] = total

        for out, (acc, hops, terms) in zip(outs, jobs):
            if hops is None:
                for half, pieces in enumerate(terms):
                    add(out, half, pieces, accs[acc])
                continue
            if acc is None:
                out[rows, :] = jnp.zeros((TILE, 1024), jnp.float32)
            for i in range(4):
                hop = (ahead + i) % 4

                @pl.when((hop >= hops[0]) & (hop <= hops[1]))
                def _():
                    for half, pieces in enumerate(terms):
                        here = [p for p in pieces if p[3][0] == i]
                        if here:
                            add(out, half, here, out)

        return carry

    lax.fori_loop(0, outs[0].shape[0] // TILE, tile, 0, unroll=all(job[1] is None for job in jobs))


def sums(jobs, rs, k, accs):
    rows = k.shape[1]
    args = [*map(vmem, (k, *rs, *accs))]
    first = 1 + len(rs)
    return pl.pallas_call(
        functools.partial(sum_kernel, jobs, len(rs), len(accs)),
        out_shape=tuple(pltpu.VMEM((rows, 1024), jnp.float32) for _ in jobs),
        in_specs=[VM] * len(args),
        out_specs=tuple(VM for _ in jobs),
        input_output_aliases={first + acc: o for o, (acc, _, _) in enumerate(jobs) if acc is not None},
        compiler_params=params(8),
        cost_estimate=cost(10**6),
    )(*args)


def last_kernel(halves, n_r, k, *refs):
    rs, (acc, other, out, buf, sems) = refs[:n_r], refs[n_r:]
    copies = []
    for t in range(acc.shape[0] // TILE):
        rows = slice(t * TILE, (t + 1) * TILE)
        for half, pieces in enumerate(halves):
            cols = slice(half * 512, (half + 1) * 512)
            total = acc[rows, cols] + other[rows, cols]
            for r, row0, col0, at in pieces:
                total += jnp.dot(
                    k[root_index(*at), rows, :],
                    rs[r][row0 : row0 + 256, col0 : col0 + 512],
                    preferred_element_type=jnp.float32,
                )
            buf[rows, cols] = total
            at = (pl.ds(t * TILE, TILE), pl.ds(half * 512, 512))
            cp = pltpu.make_async_copy(buf.at[at], out.at[at], sems.at[2 * t + half])
            cp.start()
            copies.append(cp)
    for cp in copies:
        cp.wait()


def last(halves, rs, k, acc, other):
    rows = k.shape[1]
    args = [*map(vmem, (k, *rs, acc, other))]
    return pl.pallas_call(
        functools.partial(last_kernel, halves, len(rs)),
        out_shape=jax.ShapeDtypeStruct((rows, 1024), jnp.float32),
        in_specs=[VM] * len(args),
        out_specs=ANY,
        scratch_shapes=[pltpu.VMEM((rows, 1024), jnp.float32), pltpu.SemaphoreType.DMA((2 * (rows // TILE),))],
        compiler_params=params(8),
        cost_estimate=cost(10**6),
    )(*args)


def shards(library_bits, library_count, landmark_bits, landmark_count, inverse_root):
    core = lax.axis_index("lmk") % NC
    mine = lax.dynamic_slice_in_dim(inverse_root, core * 256, 256, 0)
    theirs = send(lax.dynamic_slice_in_dim(inverse_root, (1 - core) * 256, 256, 0), "core")
    row_scale = 0.9 * library_count.astype(jnp.float32)[:, None]
    col_scale = 0.1 * landmark_count.astype(jnp.float32)[None, :]
    row_bits, col_bits, token = load(library_bits, landmark_bits)
    theirs, swapped = lax.optimization_barrier((theirs, pick(landmark_bits)))
    own = [theirs, mine]
    first = [[[], []] for _ in range(2)]
    second = [[[], []] for _ in range(2)]
    for s in range(2):
        first[s][0].append(send(own[s], "y"))
        first[s][1].append(send(own[s], "z"))
    ks = [tversky(row_bits, row_scale, col_bits, col_scale, send(swapped, "core"))]

    def second_terms(hop, p):
        return [[(p, 256 * m, 0, (hop, m + 1)) for m in range(3)], [(p + 1, 256 * m, 0, (m + 1, hop)) for m in range(3)]]

    def first_terms(s, p):
        rs = [own[s], *first[s][0], *first[s][1], second[s][0][0], second[s][1][0]]
        where = [(0, 0), (0, 1), (0, 2), (0, 3), (1, 0), (2, 0), (3, 0)]
        more = second_terms(1, p + 7)
        return [[(p + n, 0, 512 * h, at) for n, at in enumerate(where)] + more[h] for h in range(2)], rs

    for step in range(10):
        s, hop = step % 2, step // 2
        rings = (first if hop < 3 else second)[s]
        ready = [rings[0][hop % 3], rings[1][hop % 3]]
        if step == 8:
            k = place([0, 1, 2], ks[:3])
            terms, rs = first_terms(0, 0)
            (acc,) = sums([(None, (0, 2), terms)], rs, k, [])
            ready.append(acc)
        if step == 9:
            terms, rs = first_terms(1, 0)
            jobs = [(None, (0, 2), terms), (0, (0, 2), second_terms(2, len(rs)))]
            other, acc = sums(jobs, [*rs, second[0][0][1], second[0][1][1]], k, [acc])
            ready.append(other)
        if step in (X1, X2):
            ready.append(ks[-1])
        token, *done = tie(token, *ready, flops=TIES[step] * 10**9)
        rings[0][hop % 3], rings[1][hop % 3] = done[:2]
        if step == 8:
            acc = done[2]
        if step == 9:
            other = done[2]
        if step in (X1, X2):
            ks[-1] = done[2]
        if hop < 2:
            rings[0].append(send(done[0], "y"))
            rings[1].append(send(done[1], "z"))
        elif hop == 2:
            left = jnp.concatenate([q[:, :512] for q in rings[0]])
            right = jnp.concatenate([q[:, 512:] for q in rings[1]])
            second[s][0].append(send(left, "z"))
            second[s][1].append(send(right, "y"))
        elif hop < 5:
            rings[0].append(send(done[0], "z"))
            rings[1].append(send(done[1], "y"))
        if step in (0, X1, X2):
            ks.append(send(ks[-1], "x"))

    k = place([3], ks[3:], k)
    terms, rs = first_terms(0, 0)
    more = second_terms(2, len(rs))
    terms = [terms[h] + more[h] for h in range(2)]
    (acc,) = sums([(0, (3, 3), terms)], [*rs, second[0][0][1], second[0][1][1]], k, [acc])
    (acc,) = sums([(0, None, second_terms(3, 0))], [second[0][0][2], second[0][1][2]], k, [acc])
    theirs = send(acc, "core")
    terms, rs = first_terms(1, 0)
    (other,) = sums([(0, (3, 3), terms)], rs, k, [other])
    (other,) = sums([(0, None, second_terms(2, 0))], [second[1][0][1], second[1][1][1]], k, [other])
    tail = tie(second[1][0][2], second[1][1][2], flops=TAIL)
    return last(second_terms(3, 0), tail, k, other, theirs)


def solution(mesh):
    placed = (P("lib", None), P("lib"), P("lmk", None), P("lmk"), P("lib", "lmk"))
    return jax.shard_map(
        shards, mesh=mesh, in_specs=placed, out_specs=P("lib", "lmk"), check_vma=False
    )
```
